512 devices in a mesh: group: 4 (over y_hi), seq: 32 (over x, z), head: 4 (over y_lo, core).
Axes of the slice: x: 4, y: 8 (y_hi: 4, y_lo: 2; y = y_hi * 2 + y_lo), z: 8, core: 2. Of those that a mesh axis runs over, the one named last changes fastest.
Arguments:
- latents: bfloat16 [4096, 64], P('seq'), may hold values from -6 to 6
- noise: bfloat16 [4096, 64], P('seq'), may hold values from -6 to 6
- step: int32 [1], replicated, may hold values from 50 to 950
- stream: bfloat16 [4096, 5120], P('seq'), may hold values from -6 to 6
- patch_embed_weight: bfloat16 [64, 5120], replicated, may hold values from -0.75 to 0.75
- prenorm_gain_vector: float32 [5120], replicated, may hold values from 0.5 to 1.5
- query_matrix: bfloat16 [5120, 4096], P('seq', ('group', 'head')), may hold values from -0.08385255 to 0.08385255
- key_matrix: bfloat16 [5120, 4096], P('seq', ('group', 'head')), may hold values from -1.0481569 to 1.0481569
- value_matrix: bfloat16 [5120, 4096], P('seq', ('group', 'head')), may hold values from -0.078125 to 0.078125
- output_matrix: bfloat16 [4096, 5120], P(('group', 'head'), 'seq'), may hold values from -0.09375 to 0.09375
- velocity_readout_weight: bfloat16 [64, 5120], replicated, may hold values from -0.078125 to 0.078125
- adapter_query_down: bfloat16 [5120, 128], P('seq'), may hold values from -0.078125 to 0.078125
- adapter_query_up: bfloat16 [128, 4096], P(None, ('group', 'head')), may hold values from -0.5 to 0.5
- adapter_output_down: bfloat16 [4096, 128], P(('group', 'head')), may hold values from -0.09375 to 0.09375
- adapter_output_up: bfloat16 [128, 5120], replicated, may hold values from -0.5 to 0.5
Outputs:
- latent_grad: float32 [4096, 64], P('seq')
The draws below stay inside these ranges and needn't reach their ends.
All inputs are finite; a program needn't handle non-finite values. Where the reference program divides by a largest or mean magnitude, that divisor is 1e-20 or more.
Results may differ from the reference program's by a relative error of at most 0.015.
Values may be sent and summed in bfloat16 or wider, within the bound.
A program may use at most 64 MiB of HBM per device.

```python
import jax
import jax.numpy as jnp
from jax import lax

MODEL_WIDTH = 5120
ATTENTION_HEADS = 32
HEAD_SIZE = 128
CHANNELS = 64
ADAPTER_RANK = 128
SEQ_LEN = 4096


def paired_draw(key):
    first = jnp.clip(jax.random.normal(jax.random.fold_in(key, 7), (MODEL_WIDTH, ATTENTION_HEADS * HEAD_SIZE), jnp.float32), -6.0, 6.0)
    second = jnp.clip(jax.random.normal(jax.random.fold_in(key, 8), (MODEL_WIDTH, ATTENTION_HEADS * HEAD_SIZE), jnp.float32), -6.0, 6.0)
    return (first * MODEL_WIDTH ** (-0.5), second * MODEL_WIDTH ** (-0.5))


def draw_query_matrix(key, part):
    first, second = paired_draw(key)
    return first.astype(jnp.bfloat16)


def draw_key_matrix(key, part):
    first, second = paired_draw(key)
    return second.astype(jnp.bfloat16)


def block_scale(rng, extent, shards, low, top_value):
    gain, own = 1.0, jax.random.fold_in(rng, 6)
    for dim, parts in shards:
        steps = jnp.exp(jax.random.uniform(jax.random.fold_in(own, dim), (parts,), jnp.float32, low / len(shards), top_value / len(shards)))
        gain = gain * jnp.repeat(steps, extent[dim] // parts).reshape([-1 if axis == dim else 1 for axis in range(len(extent))])
    return gain


def normal_values(key, dims, width, most, split=(), kind=jnp.bfloat16):
    gain = block_scale(key, dims, split, -0.22, 0.18) if split else 1.0
    array = jax.random.normal(key, dims, jnp.float32) * width * gain
    return jnp.minimum(jnp.maximum(array, -most), most).astype(kind)


def setup_inputs(seed: int = 0) -> dict:
    key_of = jax.random.split(jax.random.key(seed), 16)
    return {
        "latents": normal_values(key_of[0], (SEQ_LEN, CHANNELS), 1.0, 6.0, ((0, 32),)),
        "noise": normal_values(key_of[1], (SEQ_LEN, CHANNELS), 1.0, 6.0, ((0, 32),)),
        "step": jax.random.randint(key_of[2], (1,), 50, 951).astype(jnp.int32),
        "stream": normal_values(key_of[3], (SEQ_LEN, MODEL_WIDTH), 1.0, 6.0, ((0, 32),)),
        "patch_embed_weight": normal_values(key_of[4], (CHANNELS, MODEL_WIDTH), CHANNELS ** -0.5, 0.75),
        "prenorm_gain_vector": jnp.clip(1.0 + 0.1 * jax.random.normal(key_of[5], (MODEL_WIDTH,), jnp.float32), 0.5, 1.5),
        "query_matrix": draw_query_matrix(jax.random.fold_in(key_of[15], 71), 0),
        "key_matrix": draw_key_matrix(jax.random.fold_in(key_of[15], 71), 0),
        "value_matrix": normal_values(key_of[8], (MODEL_WIDTH, ATTENTION_HEADS * HEAD_SIZE), MODEL_WIDTH ** -0.5, 0.078125, ((0, 32), (1, 16))),
        "output_matrix": normal_values(key_of[9], (ATTENTION_HEADS * HEAD_SIZE, MODEL_WIDTH), (ATTENTION_HEADS * HEAD_SIZE) ** -0.5, 0.09375, ((0, 16), (1, 32))),
        "velocity_readout_weight": normal_values(key_of[10], (CHANNELS, MODEL_WIDTH), MODEL_WIDTH ** -0.5, 0.078125),
        "adapter_query_down": normal_values(key_of[11], (MODEL_WIDTH, ADAPTER_RANK), MODEL_WIDTH ** -0.5, 0.078125, ((0, 32),)),
        "adapter_query_up": normal_values(key_of[12], (ADAPTER_RANK, ATTENTION_HEADS * HEAD_SIZE), ADAPTER_RANK ** -0.5, 0.5, ((1, 16),)),
        "adapter_output_down": normal_values(key_of[13], (ATTENTION_HEADS * HEAD_SIZE, ADAPTER_RANK), (ATTENTION_HEADS * HEAD_SIZE) ** -0.5, 0.09375, ((0, 16),)),
        "adapter_output_up": normal_values(key_of[14], (ADAPTER_RANK, MODEL_WIDTH), ADAPTER_RANK ** -0.5, 0.5),
    }


def attend_head(items):
    first, second, keys, values = items
    outs = []
    for query in (first, second):
        scores = jnp.dot(query, keys.T, preferred_element_type=jnp.float32)
        top = lax.optimization_barrier(jnp.max(scores, axis=-1, keepdims=True))
        weights = jnp.exp(scores - top)
        total = lax.optimization_barrier(jnp.sum(weights, axis=-1, keepdims=True))
        outs.append(jnp.dot(weights.astype(jnp.bfloat16), values, preferred_element_type=jnp.float32) / total)
    return jnp.stack(outs).astype(jnp.bfloat16)

def split_heads(matrix):
    return matrix.reshape(SEQ_LEN, ATTENTION_HEADS, HEAD_SIZE).transpose(1, 0, 2)

def reference(latents, noise, step, stream, patch_embed_weight, prenorm_gain_vector, query_matrix, key_matrix, value_matrix, output_matrix, velocity_readout_weight, adapter_query_down, adapter_query_up, adapter_output_down, adapter_output_up):
    level = (step[0].astype(jnp.float32) + 1.0) / 1000.0
    sigma = 5.0 * level / (1.0 + 4.0 * level)
    noisy = ((1.0 - sigma) * latents.astype(jnp.float32) + sigma * noise.astype(jnp.float32)).astype(jnp.bfloat16)
    hidden = (stream.astype(jnp.float32) + jnp.dot(noisy, patch_embed_weight, preferred_element_type=jnp.float32)).astype(jnp.bfloat16)
    hidden_wide = hidden.astype(jnp.float32)
    normalized_tokens = (hidden_wide * lax.rsqrt(lax.optimization_barrier(jnp.mean(hidden_wide * hidden_wide, axis=-1, keepdims=True)) + 1e-06) * prenorm_gain_vector).astype(jnp.bfloat16)
    logit_scale = HEAD_SIZE ** (-0.5)
    base_query_rows = jnp.dot(normalized_tokens, query_matrix, preferred_element_type=jnp.float32)
    adapter_hidden_rows = jnp.dot(normalized_tokens, adapter_query_down, preferred_element_type=jnp.float32).astype(jnp.bfloat16)
    adapter_query_delta = jnp.dot(adapter_hidden_rows, adapter_query_up, preferred_element_type=jnp.float32)
    queries = (base_query_rows * logit_scale).astype(jnp.bfloat16)
    fake_query_rows = ((base_query_rows + adapter_query_delta) * logit_scale).astype(jnp.bfloat16)
    keys = jnp.dot(normalized_tokens, key_matrix, preferred_element_type=jnp.float32).astype(jnp.bfloat16)
    values = jnp.dot(normalized_tokens, value_matrix, preferred_element_type=jnp.float32).astype(jnp.bfloat16)
    heads_out = lax.map(attend_head, (split_heads(queries), split_heads(fake_query_rows), split_heads(keys), split_heads(values)))
    attn = heads_out.transpose(1, 2, 0, 3).reshape(2, SEQ_LEN, ATTENTION_HEADS * HEAD_SIZE)
    blended_heads_whole = jnp.dot(output_matrix, velocity_readout_weight.T, preferred_element_type=jnp.float32)
    adapter_readout_delta = jnp.dot(adapter_output_up, velocity_readout_weight.T, preferred_element_type=jnp.float32).astype(jnp.bfloat16)
    mix = blended_heads_whole.astype(jnp.bfloat16)
    fake_head_blend = (blended_heads_whole + jnp.dot(adapter_output_down, adapter_readout_delta, preferred_element_type=jnp.float32)).astype(jnp.bfloat16)
    base = jnp.dot(hidden, velocity_readout_weight.T, preferred_element_type=jnp.float32)
    v_real = base + jnp.dot(attn[0], mix, preferred_element_type=jnp.float32)
    v_fake = base + jnp.dot(attn[1], fake_head_blend, preferred_element_type=jnp.float32)
    noisy_wide = noisy.astype(jnp.float32)
    x0_real = noisy_wide - sigma * v_real
    x0_fake = noisy_wide - sigma * v_fake
    weight = jnp.mean(jnp.abs(latents.astype(jnp.float32) - x0_real))
    return (x0_fake - x0_real) / weight
```

```python
import functools

import jax
import jax.numpy as jnp
from jax import lax
from jax.experimental import pallas as pl
from jax.experimental.pallas import tpu as pltpu
from jax.sharding import PartitionSpec as P

HEAD = 128
X = 4
MESH = pl.DeviceIdType.MESH
BF16 = jnp.bfloat16
F32 = jnp.float32


def dot_t(left, right):
    return lax.dot_general(
        left, right, (((1,), (1,)), ((), ())), preferred_element_type=F32
    )


def dot(left, right):
    return jnp.dot(left, right, preferred_element_type=F32)


def kernel(
    dims,
    step_ref,
    lat_ref,
    noise_ref,
    stream_ref,
    pe_ref,
    gain_ref,
    wq_ref,
    wk_ref,
    wv_ref,
    om_ref,
    vel_ref,
    ad_ref,
    aup_ref,
    aod_ref,
    aou_ref,
    out_ref,
    hid,
    acts,
    wbuf,
    mpart,
    mpair,
    mring,
    aup_all,
    aod_all,
    pacc,
    precv,
    mhalf,
    mrecv,
    kv,
    q2,
    sc,
    mx_ref,
    l_ref,
    acc_ref,
    part,
    red,
    fin,
    err,
    errs,
    xs_send,
    xs_recv,
    a_send,
    a_recv,
    wr_send,
    wr_recv,
    d_send,
    d_recv,
    kr_send,
    kr_recv,
    kd_send,
    kd_recv,
    red_send,
    red_recv,
    fin_send,
    fin_recv,
    err_send,
    err_recv,
):
    Y, Z, YL = dims
    T, D = stream_ref.shape
    half = D // 2
    R = wq_ref.shape[0]
    C = lat_ref.shape[1]
    PT = T // (2 * Y)
    H = Z // 2
    seq = lax.axis_index("seq")
    hd = lax.axis_index("head")
    y = lax.axis_index("group") * YL + hd // 2
    c = hd % 2
    x = seq // Z
    z = seq % Z
    o = 1 - c

    def dev(xx, yy, zz, cc):
        return {"group": yy // YL, "seq": xx * Z + zz, "head": (yy % YL) * 2 + cc}

    def remote(src, dst, ssem, rsem, where):
        return pltpu.make_async_remote_copy(
            src_ref=src, dst_ref=dst, send_sem=ssem, recv_sem=rsem,
            device_id=where, device_id_type=MESH,
        )

    def arrived(ref, sem):
        pltpu.make_async_copy(ref, ref, sem).wait()

    barrier = pltpu.get_barrier_semaphore()

    def greet_plane(i, _):
        xx, yy, cc = i // (2 * Y), (i // 2) % Y, i % 2

        @pl.when(jnp.logical_not((xx == x) & (yy == y) & (cc == c)))
        def _():
            pl.semaphore_signal(barrier, inc=1, device_id=dev(xx, yy, z, cc), device_id_type=MESH)

        return 0

    def greet_seq(i, _):
        xx, zz = i // Z, i % Z

        @pl.when(zz != z)
        def _():
            pl.semaphore_signal(barrier, inc=1, device_id=dev(xx, y, zz, c), device_id_type=MESH)

        return 0

    lax.fori_loop(0, X * Y * 2, greet_plane, 0)
    lax.fori_loop(0, X * Z, greet_seq, 0)

    lo = R * seq // 128
    window = vel_ref[:, pl.ds(pl.multiple_of(lo * 128, 128), 256)].astype(F32)
    off = R * seq - lo * 128
    turned = pltpu.roll(window, lax.rem(256 - off, 256), 1).astype(BF16)
    mp = dot_t(turned[:, :R], om_ref[...])
    mpart[0] = mp[:, :HEAD]
    mpart[1] = mp[:, HEAD:]

    pl.semaphore_wait(barrier, X * Y * 2 - 1 + X * (Z - 1))

    weights = (wq_ref, wk_ref, wv_ref, ad_ref)
    xslot = x % 2
    myrows = pl.ds(pl.multiple_of(R * z, 16), R)

    def exchange(i):
        pairs = []
        for n, w in enumerate(weights):
            src = w if n == 3 else w.at[:, pl.ds(HEAD * i, HEAD)]
            pairs.append((src, wbuf.at[xslot, myrows, pl.ds(HEAD * n, HEAD)]))
        pairs.append((mpart.at[i], mpair.at[xslot]))
        return pairs

    for i in range(2):
        j = 2 * c + i
        for n, (src, dst) in enumerate(exchange(i)):

            @pl.when(j != x)
            def _():
                remote(src, dst, xs_send.at[i, n], xs_recv.at[xslot, n], dev(j, y, z, x // 2)).start()

            @pl.when(j == x)
            def _():
                pltpu.make_async_copy(src, dst, xs_recv.at[xslot, n]).start()

    other = dev(x, y, z, o)
    up = remote(aup_ref, aup_all.at[c], d_send.at[0], d_recv.at[0], other)
    od = remote(aod_ref, aod_all.at[c], d_send.at[1], d_recv.at[1], other)
    up.start()
    od.start()
    aup_all[c] = aup_ref[...]
    aod_all[c] = aod_ref[...]

    level = (jnp.full((1, 1), step_ref[0], jnp.int32).astype(F32) + 1.0) / 1000.0
    sigma = 5.0 * level / (1.0 + 4.0 * level)
    noisy = ((1.0 - sigma) * lat_ref[...].astype(F32) + sigma * noise_ref[...].astype(F32)).astype(BF16)
    wide = 640 if D % 640 == 0 else D
    total = jnp.zeros((T, 1), F32)
    for k in range(D // wide):
        cols = slice(k * wide, (k + 1) * wide)
        h = (stream_ref[:, cols].astype(F32) + dot(noisy, pe_ref[:, cols])).astype(BF16)
        hid[:, cols] = h
        hw = h.astype(F32)
        total = total + jnp.sum(hw * hw, axis=1, keepdims=True)
    scale = lax.rsqrt(total / D + 1e-06)
    for k in range(half // wide):
        at = pl.ds(pl.multiple_of(c * half + k * wide, 128), wide)
        n = (hid[:, at].astype(F32) * scale * gain_ref[:, at]).astype(BF16)
        acts[x, :, k * wide : (k + 1) * wide] = n

    sends = []
    for d in range(1, X):
        xx = (x + d) % X
        sends.append(remote(acts.at[x], acts.at[x], a_send.at[d], a_recv.at[x], dev(xx, y, z, c)))
    for s in sends:
        s.start()

    for s in range(2):
        for n in range(4):
            arrived(wbuf.at[s, myrows, pl.ds(HEAD * n, HEAD)], xs_recv.at[s, n])
        arrived(mpair.at[s], xs_recv.at[s, 4])
    mring[z] = mpair[0] + mpair[1]

    right, left = dev(x, y, (z + 1) % Z, c), dev(x, y, (z + Z - 1) % Z, c)

    def ring(pieces, ssem, rsem, t):
        last = t == H - 1
        zr, zl = (z + Z - t) % Z, (z + t) % Z
        copies = []
        for n, piece in enumerate(pieces):
            copies.append(remote(piece(zr, 0 if last else None), piece(zr, 0 if last else None),
                                 ssem.at[0, t, n], rsem.at[0, t, n], right))
            copies.append(remote(piece(zl, 1 if last else None), piece(zl, 1 if last else None),
                                 ssem.at[1, t, n], rsem.at[1, t, n], left))
        return copies

    def came(pieces, rsem, t):
        last = t == H - 1
        zr, zl = (z + Z - t - 1) % Z, (z + t + 1) % Z
        for n, piece in enumerate(pieces):
            arrived(piece(zr, 0 if last else None), rsem.at[0, t, n])
            arrived(piece(zl, 1 if last else None), rsem.at[1, t, n])

    def wpiece(zz, part_):
        rows = pl.ds(pl.multiple_of(R * zz, 16), R)
        return wbuf.at[:, rows, :] if part_ is None else wbuf.at[part_, rows, :]

    def mpiece(zz, part_):
        return mring.at[zz] if part_ is None else mring.at[zz, pl.ds(part_ * C // 2, C // 2), :]

    wring = []
    for t in range(H):
        if t:
            came((wpiece, mpiece), wr_recv, t - 1)
        copies = ring((wpiece, mpiece), wr_send, wr_recv, t)
        for s in copies:
            s.start()
        wring += copies
        if t == 0:
            base = dot_t(hid[...], vel_ref[...])
            readout = dot_t(vel_ref[...], aou_ref[...]).astype(BF16)
    came((wpiece, mpiece), wr_recv, H - 1)
    for d in range(1, X):
        arrived(acts.at[0], a_recv.at[(x + d) % X])

    zr_ = Z * R
    for b in range(X):
        pacc[b * T : (b + 1) * T] = dot(acts[b, :, :zr_], wbuf[0]) + dot(acts[b, :, zr_:], wbuf[1])
    mh = mring[0]
    for zz in range(1, Z):
        mh = mh + mring[zz]
    mhalf[...] = mh
    give = remote(pacc.at[pl.ds(pl.multiple_of(2 * T * o, 16), 2 * T)], precv, d_send.at[2], d_recv.at[2], other)
    givem = remote(mhalf, mrecv, d_send.at[3], d_recv.at[3], other)
    give.start()
    givem.start()
    up.wait()
    od.wait()
    give.wait()
    givem.wait()
    mine = pl.ds(pl.multiple_of(2 * T * c, 16), 2 * T)
    proj = pacc[mine] + precv[...]
    kv[c, z] = proj[:, HEAD : 3 * HEAD].astype(BF16)

    def kpiece(zz, part_):
        return kv.at[c, zz] if part_ is None else kv.at[c, zz, pl.ds(part_ * T, T), :]

    def across(zz):
        s = remote(kv.at[c, zz], kv.at[c, zz], kd_send.at[zz], kd_recv.at[zz], other)
        s.start()
        return s

    kring = []
    cross = []
    for t in range(H):
        if t:
            came((kpiece,), kr_recv, t - 1)
        copies = ring((kpiece,), kr_send, kr_recv, t)
        for s in copies:
            s.start()
        kring += copies
        if t == 0:
            cross.append(across(z))
            lora = proj[:, 3 * HEAD :].astype(BF16)
            lane = pl.ds(pl.multiple_of(HEAD * (x % 2), HEAD), HEAD)
            delta = dot(lora, aup_all[x // 2, :, lane])
            logit = HEAD ** (-0.5)
            q2[: 2 * T] = (proj[:, :HEAD] * logit).astype(BF16)
            q2[2 * T :] = ((proj[:, :HEAD] + delta) * logit).astype(BF16)
            mixw = mhalf[...] + mrecv[...]
            mix = mixw.astype(BF16)
            fmix = (mixw + dot_t(readout, aod_all[x // 2, lane, :])).astype(BF16)
            zero = jnp.zeros_like(mix)
            mix = jnp.concatenate([mix, zero], axis=0)
            fmix = jnp.concatenate([zero, fmix], axis=0)
        else:
            cross.append(across((z + Z - t) % Z))
            cross.append(across((z + t) % Z))
    came((kpiece,), kr_recv, H - 1)
    cross.append(across((z + H) % Z))
    for zz in range(Z):
        arrived(kv.at[o, zz], kd_recv.at[zz])

    mx_ref[...] = jnp.full(mx_ref.shape, -jnp.inf, F32)

    def scores(n, _):
        s = dot_t(q2[...], kv[n // Z, n % Z, :, :HEAD])
        sc[n] = s
        m = mx_ref[...]
        for g in range(2 * T // HEAD):
            m = jnp.maximum(m, s[:, g * HEAD : (g + 1) * HEAD])
        mx_ref[...] = m
        return 0

    lax.fori_loop(0, 2 * Z, scores, 0)
    top = jnp.max(mx_ref[...], axis=1, keepdims=True)
    mx_ref[...] = jnp.broadcast_to(top, mx_ref.shape)
    l_ref[...] = jnp.zeros(l_ref.shape, F32)
    acc_ref[...] = jnp.zeros(acc_ref.shape, F32)

    def gather(n, _):
        m = mx_ref[...]
        s = sc[n]
        ps = [jnp.exp(s[:, g * HEAD : (g + 1) * HEAD] - m) for g in range(2 * T // HEAD)]
        l = l_ref[...]
        for p in ps:
            l = l + p
        l_ref[...] = l
        probs = jnp.concatenate([p.astype(BF16) for p in ps], axis=1)
        acc_ref[...] += dot(probs, kv[n // Z, n % Z, :, HEAD:])
        return 0

    lax.fori_loop(0, 2 * Z, gather, 0)
    attn = (acc_ref[...] / jnp.sum(l_ref[...], axis=1, keepdims=True)).astype(BF16)
    part[...] = dot_t(attn[: 2 * T], mix) + dot_t(attn[2 * T :], fmix)

    slot = x * Y + y

    def scatter(fn_remote, fn_local):
        def body(i, _):
            b, p = i // (2 * Y), i % (2 * Y)
            xx, yy, cc = 2 * c + b, p // 2, p % 2
            src = part.at[pl.ds(pl.multiple_of(b * T + p * PT, PT), PT), :]
            me = (xx == x) & (yy == y) & (cc == c)

            @pl.when(jnp.logical_not(me))
            def _():
                fn_remote(remote(src, red.at[slot], red_send.at[i], red_recv, dev(xx, yy, z, cc)))

            if fn_local is not None:

                @pl.when(me)
                def _():
                    fn_local(pltpu.make_async_copy(src, red.at[slot], red_recv))

            return 0

        lax.fori_loop(0, 4 * Y, body, 0)

    scatter(lambda s: s.start(), lambda s: s.start())
    arrived(red, red_recv)
    pos = 2 * y + c
    acc = red[0]
    for n in range(1, X * Y):
        acc = acc + red[n]
    err[0] = acc

    def spread(fn):
        def body(d, _):
            p = (pos + d) % (2 * Y)
            fn(remote(err.at[0], fin.at[2 * Y - d], fin_send.at[d], fin_recv.at[d], dev(x, p // 2, z, p % 2)))
            return 0

        lax.fori_loop(1, 2 * Y, body, 0)

    spread(lambda s: s.start())
    fin[0] = acc
    spread(lambda s: s.wait())
    sums = jnp.concatenate([fin[(n + 2 * Y - pos) % (2 * Y)] for n in range(2 * Y)], axis=0)
    noisy_wide = noisy.astype(F32)
    x0_real = noisy_wide - sigma * (base + sums[:, :C])
    x0_fake = noisy_wide - sigma * (base + sums[:, C:])
    gap = jnp.abs(lat_ref[...].astype(F32) - x0_real)
    err[1, 0:8, 0:C] = jnp.sum(gap.reshape(T // 8, 8, C), axis=0)
    errs[0, :, 0:C] = err[1, 0:8, 0:C]
    S = X * Z

    def tell(fn):
        def body(d, _):
            s = (seq + d) % S
            fn(remote(err.at[1, pl.ds(0, 8)], errs.at[d], err_send.at[d], err_recv.at[d], {"group": lax.axis_index("group"), "seq": s, "head": hd}))
            return 0

        lax.fori_loop(1, S, body, 0)

    tell(lambda s: s.start())
    tell(lambda s: s.wait())
    tot = errs[0]
    for n in range(1, S):
        tot = tot + errs[n]
    tot = jnp.sum(jnp.sum(tot[:, :C], axis=0, keepdims=True), axis=1, keepdims=True)
    weight = tot / (T * S * C)
    out_ref[...] = (x0_fake - x0_real) / weight

    for i in range(2):
        j = 2 * c + i
        for n, (src, dst) in enumerate(exchange(i)):

            @pl.when(j != x)
            def _():
                remote(src, dst, xs_send.at[i, n], xs_recv.at[xslot, n], dev(j, y, z, x // 2)).wait_send()

    for s in sends + wring + kring + cross:
        s.wait_send()
    scatter(lambda s: s.wait_send(), None)


def local(
    latents, noise, step, stream, patch_embed_weight, prenorm_gain_vector, query_matrix,
    key_matrix, value_matrix, output_matrix, velocity_readout_weight, adapter_query_down,
    adapter_query_up, adapter_output_down, adapter_output_up, *, dims,
):
    Y, Z, YL = dims
    T, D = stream.shape
    C = latents.shape[1]
    R = query_matrix.shape[0]
    PT = max(T // (2 * Y), 8)
    H = Z // 2
    vmem = pl.BlockSpec(memory_space=pltpu.VMEM)
    dma = pltpu.SemaphoreType.DMA
    return pl.pallas_call(
        functools.partial(kernel, dims),
        out_shape=jax.ShapeDtypeStruct((T, C), F32),
        in_specs=[pl.BlockSpec(memory_space=pltpu.SMEM)] + [vmem] * 14,
        out_specs=vmem,
        scratch_shapes=[
            pltpu.VMEM((T, D), BF16),
            pltpu.VMEM((X, T, D // 2), BF16),
            pltpu.VMEM((2, Z * R, 4 * HEAD), BF16),
            pltpu.VMEM((2, C, HEAD), F32),
            pltpu.VMEM((2, C, HEAD), F32),
            pltpu.VMEM((Z, C, HEAD), F32),
            pltpu.VMEM((2, HEAD, 2 * HEAD), BF16),
            pltpu.VMEM((2, 2 * HEAD, HEAD), BF16),
            pltpu.VMEM((X * T, 4 * HEAD), F32),
            pltpu.VMEM((2 * T, 4 * HEAD), F32),
            pltpu.VMEM((C, HEAD), F32),
            pltpu.VMEM((C, HEAD), F32),
            pltpu.VMEM((2, Z, 2 * T, 2 * HEAD), BF16),
            pltpu.VMEM((4 * T, HEAD), BF16),
            pltpu.VMEM((2 * Z, 4 * T, 2 * T), F32),
            pltpu.VMEM((4 * T, HEAD), F32),
            pltpu.VMEM((4 * T, HEAD), F32),
            pltpu.VMEM((4 * T, HEAD), F32),
            pltpu.VMEM((2 * T, 2 * C), F32),
            pltpu.VMEM((X * Y, PT, 2 * C), F32),
            pltpu.VMEM((2 * Y, PT, 2 * C), F32),
            pltpu.VMEM((2, PT, 2 * C), F32),
            pltpu.VMEM((X * Z, 8, 2 * C), F32),
            dma((2, 5)), dma((2, 5)),
            dma((X,)), dma((X,)),
            dma((2, H, 2)), dma((2, H, 2)),
            dma((4,)), dma((4,)),
            dma((2, H, 1)), dma((2, H, 1)),
            dma((Z,)), dma((Z,)),
            dma((4 * Y,)), dma,
            dma((2 * Y,)), dma((2 * Y,)),
            dma((X * Z,)), dma((X * Z,)),
        ],
        compiler_params=pltpu.CompilerParams(
            collective_id=0, has_side_effects=True, vmem_limit_bytes=56 * 1024 * 1024
        ),
    )(
        step, latents, noise, stream, patch_embed_weight, prenorm_gain_vector.reshape(1, D),
        query_matrix, key_matrix, value_matrix, output_matrix, velocity_readout_weight,
        adapter_query_down, adapter_query_up, adapter_output_down, adapter_output_up,
    )


def solution(mesh):
    heads = ("group", "head")
    in_specs = (
        P("seq", None), P("seq", None), P(), P("seq", None), P(), P(),
        P("seq", heads), P("seq", heads), P("seq", heads), P(heads, "seq"),
        P(), P("seq", None), P(None, heads), P(heads, None), P(),
    )
    YL = mesh.shape["head"] // 2
    dims = (mesh.shape["group"] * YL, mesh.shape["seq"] // X, YL)
    return jax.shard_map(
        functools.partial(local, dims=dims), mesh=mesh, in_specs=in_specs,
        out_specs=P("seq", None), check_vma=False,
    )
```

```python
import functools

import jax
import jax.numpy as jnp
from jax import lax
from jax.experimental import pallas as pl
from jax.experimental.pallas import tpu as pltpu
from jax.sharding import PartitionSpec as P

HEAD = 128
X = 4
MESH = pl.DeviceIdType.MESH
BF16 = jnp.bfloat16
F32 = jnp.float32


def dot_t(left, right):
    return lax.dot_general(
        left, right, (((1,), (1,)), ((), ())), preferred_element_type=F32
    )


def dot(left, right):
    return jnp.dot(left, right, preferred_element_type=F32)


SUBS = 4


def kernel(
    dims,
    step_ref,
    lat_ref,
    noise_ref,
    stream_hbm,
    pe_hbm,
    gain_ref,
    wq_ref,
    wk_ref,
    wv_ref,
    om_ref,
    vel_hbm,
    ad_ref,
    aup_ref,
    aod_ref,
    aou_hbm,
    out_ref,
    stream_ref,
    pe_ref,
    vel_ref,
    aou_ref,
    hid,
    acts,
    wbuf,
    ext,
    wlow,
    lpack,
    mpart,
    mpair,
    aup_all,
    aod_all,
    pacc,
    precv,
    qacc,
    qrecv,
    mhalf,
    mrecv,
    loraT,
    kv,
    q2,
    top_ref,
    sum_ref,
    acc_ref,
    part,
    red,
    fin,
    err,
    errs,
    load_sem,
    xs_send,
    xs_recv,
    a_send,
    a_recv,
    ay_send,
    ay_recv,
    wr_send,
    wr_recv,
    we_send,
    we_recv,
    d_send,
    d_recv,
    lo_send,
    lo_recv,
    kr_send,
    kr_recv,
    kd_send,
    kd_recv,
    red_send,
    red_recv,
    fin_send,
    fin_recv,
    err_send,
    err_recv,
):
    Y, Z, YL = dims
    T, D = stream_ref.shape
    half = D // 2
    R = wq_ref.shape[0]
    C = lat_ref.shape[0]
    PT = T // (2 * Y)
    H = Z // 2
    G = R // 32
    LC = 16
    group = lax.axis_index("group")
    seq = lax.axis_index("seq")
    hd = lax.axis_index("head")
    y = group * YL + hd // 2
    c = hd % 2
    x = seq // Z
    z = seq % Z
    o = 1 - c

    def dev(xx, yy, zz, cc):
        return {"group": yy // YL, "seq": xx * Z + zz, "head": (yy % YL) * 2 + cc}

    def remote(src, dst, ssem, rsem, where):
        return pltpu.make_async_remote_copy(
            src_ref=src, dst_ref=dst, send_sem=ssem, recv_sem=rsem,
            device_id=where, device_id_type=MESH,
        )

    def arrived(ref, sem):
        pltpu.make_async_copy(ref, ref, sem).wait()

    loads = [
        pltpu.make_async_copy(src, dst, load_sem.at[n])
        for n, (src, dst) in enumerate(
            ((vel_hbm, vel_ref), (stream_hbm, stream_ref), (pe_hbm, pe_ref), (aou_hbm, aou_ref))
        )
    ]
    for l in loads:
        l.start()

    if LC * Y < HEAD:
        loraT[...] = jnp.zeros(loraT.shape, BF16)

    barrier = pltpu.get_barrier_semaphore()
    for i in range(X * Y * 2):
        xx, yy, cc = i // (2 * Y), (i // 2) % Y, i % 2

        @pl.when(jnp.logical_not((xx == x) & (yy == y) & (cc == c)))
        def _():
            pl.semaphore_signal(barrier, inc=1, device_id=dev(xx, yy, z, cc), device_id_type=MESH)

    for i in range(X * Z):
        xx, zz = i // Z, i % Z

        @pl.when(zz != z)
        def _():
            pl.semaphore_signal(barrier, inc=1, device_id=dev(xx, y, zz, c), device_id_type=MESH)

    loads[0].wait()
    lo = R * seq // 128
    window = vel_ref[:, pl.ds(pl.multiple_of(lo * 128, 128), 256)].astype(F32)
    off = R * seq - lo * 128
    turned = pltpu.roll(window, lax.rem(256 - off, 256), 1).astype(BF16)
    mp = dot(turned[:, :R], om_ref[...])
    mpart[0] = mp[:, :HEAD]
    mpart[1] = mp[:, HEAD:]

    low = pltpu.roll(ad_ref[...].astype(F32), lax.rem(128 - LC * y, 128), 1)
    lane = lax.broadcasted_iota(jnp.int32, (32, 128), 1)
    packed = jnp.zeros((32, 128), F32)
    for g in range(G):
        turned_low = low[32 * g : 32 * (g + 1)]
        if g:
            turned_low = pltpu.roll(turned_low, LC * g, 1)
        packed = jnp.where((lane >= LC * g) & (lane < LC * (g + 1)), turned_low, packed)
    lpack[...] = packed.astype(BF16)

    pl.semaphore_wait(barrier, X * Y * 2 - 1 + X * (Z - 1))

    xslot = x % 2
    myrows = pl.ds(pl.multiple_of(R * z, 16), R)

    def exchange(i):
        pairs = []
        for n, w in enumerate((wq_ref, wk_ref, wv_ref)):
            pairs.append((w.at[:, pl.ds(HEAD * i, HEAD)], wbuf.at[xslot, myrows, pl.ds(HEAD * n, HEAD)]))
        pairs.append((lpack, ext.at[z, pl.ds(pl.multiple_of(32 * xslot, 16), 32), :]))
        pairs.append((mpart.at[i], mpair.at[xslot]))
        return pairs

    for i in range(2):
        j = 2 * c + i
        for n, (src, dst) in enumerate(exchange(i)):

            @pl.when(j != x)
            def _():
                remote(src, dst, xs_send.at[i, n], xs_recv.at[xslot, n], dev(j, y, z, x // 2)).start()

            @pl.when(j == x)
            def _():
                pltpu.make_async_copy(src, dst, xs_recv.at[xslot, n]).start()

    other = dev(x, y, z, o)
    up = remote(aup_ref, aup_all.at[c], d_send.at[0], d_recv.at[0], other)
    od = remote(aod_ref, aod_all.at[c], d_send.at[1], d_recv.at[1], other)
    up.start()
    od.start()
    aup_all[c] = aup_ref[...]
    aod_all[c] = aod_ref[...]

    level = (jnp.full((1, 1), step_ref[0], jnp.int32).astype(F32) + 1.0) / 1000.0
    sigma = 5.0 * level / (1.0 + 4.0 * level)
    noisyT = ((1.0 - sigma) * lat_ref[...].astype(F32) + sigma * noise_ref[...].astype(F32)).astype(BF16)
    noisy_wide = noisyT.astype(F32)
    noisy = noisy_wide.T.astype(BF16)
    loads[1].wait()
    loads[2].wait()
    wide = 640 if D % 640 == 0 else D
    total = jnp.zeros((T, 1), F32)
    for k in range(D // wide):
        cols = slice(k * wide, (k + 1) * wide)
        h = (stream_ref[:, cols].astype(F32) + dot(noisy, pe_ref[:, cols])).astype(BF16)
        hid[:, cols] = h
        hw = h.astype(F32)
        total = total + jnp.sum(hw * hw, axis=1, keepdims=True)
    scale = lax.rsqrt(total / D + 1e-06)
    for k in range(half // wide):
        at = pl.ds(pl.multiple_of(c * half + k * wide, 128), wide)
        n = (hid[:, at].astype(F32) * scale * gain_ref[:, at]).astype(BF16)
        acts[x, :, k * wide : (k + 1) * wide] = n

    YT = T // Y
    xo = (x + 2) % X

    def yrows(block, yy):
        return acts.at[block, pl.ds(pl.multiple_of(YT * yy, 16), YT), :]

    sends = [remote(yrows(x, y), yrows(x, y), a_send.at[2], a_recv.at[2], dev(xo, y, z, c))]
    for d in (1, 3):
        sends.append(remote(acts.at[x], acts.at[x], a_send.at[d], a_recv.at[d], dev((x + d) % X, y, z, c)))
    for s in sends:
        s.start()

    for s in range(2):
        for n in range(3):
            arrived(wbuf.at[s, myrows, pl.ds(HEAD * n, HEAD)], xs_recv.at[s, n])
        arrived(ext.at[z, pl.ds(32 * s, 32), :], xs_recv.at[s, 3])
        arrived(mpair.at[s], xs_recv.at[s, 4])
    ext[z, 64 : 64 + C] = (mpair[0] + mpair[1]).astype(BF16)

    right, left = dev(x, y, (z + 1) % Z, c), dev(x, y, (z + Z - 1) % Z, c)

    def ring(piece, parts, ssem, rsem, t, extra=None):
        turns = [
            (piece(((z + Z - t) % Z, (z + t) % Z)[way], n), way, ssem.at[way, t, n], rsem.at[way, t, n],
             rsem.at[way, t - 1, n] if t else None, t < H - 1 or n // (parts // 2) == way)
            for n in range(parts)
            for way in range(2)
        ]
        if extra is not None:
            ebox, es, er = extra
            turns[2:2] = [
                (ebox(((z + Z - t) % Z, (z + t) % Z)[way], 0), way, es.at[way, t], er.at[way, t],
                 er.at[way, t - 1] if t else None, t < H - 1 or way == 0)
                for way in range(2)
            ]
        started = []
        for ref, way, ss, rs, before, goes in turns:
            if goes:
                if t:
                    arrived(ref, before)
                s = remote(ref, ref, ss, rs, (right, left)[way])
                s.start()
                started.append(s)
        for ref, way, ss, rs, before, goes in turns:
            if t and not goes:
                arrived(ref, before)
        return started

    def last(piece, parts, rsem, extra=None):
        zz = (z + H) % Z
        for n in range(parts):
            arrived(piece(zz, n), rsem.at[n // (parts // 2), H - 1, n])
        if extra is not None:
            arrived(extra[0](zz, 0), extra[2].at[0, H - 1])

    def wpiece(zz, n):
        return wbuf.at[n // 2, pl.ds(pl.multiple_of(R * zz + R // 2 * (n % 2), 16), R // 2), :]

    def epiece(zz, n):
        return ext.at[zz]

    side = (epiece, we_send, we_recv)
    wring = ring(wpiece, SUBS, wr_send, wr_recv, 0, side)

    arrived(yrows(xo, y), a_recv.at[2])
    for d in range(1, Y):
        s = remote(yrows(xo, y), yrows(xo, y), ay_send.at[d], ay_recv.at[d], dev(x, (y + d) % Y, z, c))
        s.start()
        sends.append(s)

    baseT = dot_t(vel_ref[...], hid[...])
    loads[3].wait()
    readout = dot_t(vel_ref[...], aou_ref[...]).astype(BF16)
    for t in range(1, H):
        wring += ring(wpiece, SUBS, wr_send, wr_recv, t, side)
    last(wpiece, SUBS, wr_recv, side)
    arrived(acts.at[0], a_recv.at[1])
    arrived(acts.at[0], a_recv.at[3])
    for d in range(1, Y):
        arrived(yrows(xo, y), ay_recv.at[d])

    ZR = Z * R
    theirs = pl.ds(pl.multiple_of(2 * T * o, 16), 2 * T)
    mine = pl.ds(pl.multiple_of(2 * T * c, 16), 2 * T)
    for b in range(X):
        pacc[b * T : (b + 1) * T] = dot(acts[b, :, :ZR], wbuf[0, :, HEAD:]) + dot(acts[b, :, ZR:], wbuf[1, :, HEAD:])
    give = remote(pacc.at[theirs], precv, d_send.at[2], d_recv.at[2], other)
    give.start()

    mh = jnp.zeros((C, HEAD), F32)
    for zz in range(Z):
        mh = mh + ext[zz, 64 : 64 + C].astype(F32)
        for s in range(2):
            piece = ext[zz, 32 * s : 32 * (s + 1)].astype(F32)
            for g in range(G):
                rows = pltpu.roll(piece, 128 - LC * g, 1) if g else piece
                wlow[s, R * zz + 32 * g : R * zz + 32 * (g + 1)] = rows.astype(BF16)
    mhalf[...] = mh
    givem = remote(mhalf, mrecv, d_send.at[3], d_recv.at[3], other)
    givem.start()
    give.wait_recv()
    kv[c, z] = (pacc[mine] + precv[...]).astype(BF16)

    def kpiece(zz, n):
        return kv.at[c, zz, pl.ds(n * (2 * T // SUBS), 2 * T // SUBS), :]

    def across(zz):
        s = remote(kv.at[c, zz], kv.at[c, zz], kd_send.at[zz], kd_recv.at[zz], other)
        s.start()
        return s

    kring = ring(kpiece, SUBS, kr_send, kr_recv, 0)
    cross = [across(z)]

    for b in range(X):
        qacc[b * T : (b + 1) * T, :HEAD] = dot(acts[b, :, :ZR], wbuf[0, :, :HEAD]) + dot(acts[b, :, ZR:], wbuf[1, :, :HEAD])
        qacc[b * T : (b + 1) * T, HEAD:] = dot(acts[b, :, :ZR], wlow[0]) + dot(acts[b, :, ZR:], wlow[1])
    giveq = remote(qacc.at[theirs], qrecv, d_send.at[4], d_recv.at[4], other)
    giveq.start()
    up.wait()
    od.wait()
    givem.wait()
    mixw = mhalf[...] + mrecv[...]
    mix = mixw.astype(BF16)
    at = pl.ds(pl.multiple_of(HEAD * (x % 2), HEAD), HEAD)
    fmix = (mixw + dot_t(readout, aod_all[x // 2, at, :])).astype(BF16)
    zero = jnp.zeros_like(mix)
    mix = jnp.concatenate([mix, zero], axis=0)
    fmix = jnp.concatenate([zero, fmix], axis=0)
    giveq.wait()
    qsum = qacc[mine] + qrecv[...]
    lrows = pl.ds(pl.multiple_of(LC * y, 16), LC)
    loraT[lrows, :] = qsum[:, HEAD:].T[:LC].astype(BF16)
    for d in range(1, Y):
        s = remote(loraT.at[lrows], loraT.at[lrows], lo_send.at[d], lo_recv.at[d], dev(x, (y + d) % Y, z, c))
        s.start()
        sends.append(s)
    logit = HEAD ** (-0.5)
    q2[: 2 * T] = (qsum[:, :HEAD] * logit).astype(BF16)
    top_ref[...] = jnp.full(top_ref.shape, -jnp.inf, F32)
    sum_ref[...] = jnp.zeros(sum_ref.shape, F32)
    acc_ref[...] = jnp.zeros(acc_ref.shape, F32)

    def attend(cc, zz):
        for st in range(2):
            rows = slice(2 * T * st, 2 * T * (st + 1))
            s = dot_t(q2[rows], kv[cc, zz, :, :HEAD])
            best = s[:, :HEAD]
            for g in range(1, 2 * T // HEAD):
                best = jnp.maximum(best, s[:, g * HEAD : (g + 1) * HEAD])
            old = top_ref[rows]
            new = jnp.maximum(old, jnp.max(best, axis=1, keepdims=True))
            fade = jnp.exp(old - new)
            ps = [jnp.exp(s[:, g * HEAD : (g + 1) * HEAD] - new) for g in range(2 * T // HEAD)]
            l = sum_ref[rows] * fade
            for p in ps:
                l = l + p
            sum_ref[rows] = l
            top_ref[rows] = new
            probs = jnp.concatenate([p.astype(BF16) for p in ps], axis=1)
            acc_ref[rows] = acc_ref[rows] * fade + dot(probs, kv[cc, zz, :, HEAD:])

    def attend_both(zz):
        attend(c, zz)
        arrived(kv.at[o, zz], kd_recv.at[zz])
        attend(o, zz)

    for t in range(1, H):
        kring += ring(kpiece, SUBS, kr_send, kr_recv, t)
        cross.append(across((z + Z - t) % Z))
        cross.append(across((z + t) % Z))
        if t == 1:
            for d in range(1, Y):
                arrived(loraT.at[lrows], lo_recv.at[d])
            delta = lax.dot_general(
                loraT[...], aup_all[x // 2, :, at], (((0,), (0,)), ((), ())), preferred_element_type=F32
            )
            q2[2 * T :] = ((qsum[:, :HEAD] + delta) * logit).astype(BF16)
            attend_both(z)
        else:
            attend_both((z + Z - t + 1) % Z)
            attend_both((z + t - 1) % Z)
    if H == 1:
        for d in range(1, Y):
            arrived(loraT.at[lrows], lo_recv.at[d])
        delta = lax.dot_general(
            loraT[...], aup_all[x // 2, :, at], (((0,), (0,)), ((), ())), preferred_element_type=F32
        )
        q2[2 * T :] = ((qsum[:, :HEAD] + delta) * logit).astype(BF16)
        attend_both(z)
    else:
        attend_both((z + Z - H + 1) % Z)
        attend_both((z + H - 1) % Z)
    last(kpiece, SUBS, kr_recv)
    cross.append(across((z + H) % Z))
    attend_both((z + H) % Z)

    attn = (acc_ref[...] / jnp.sum(sum_ref[...], axis=1, keepdims=True)).astype(BF16)
    part[...] = dot_t(attn[: 2 * T], mix) + dot_t(attn[2 * T :], fmix)

    slot = x * Y + y

    def scatter(fn_remote, fn_local):
        for i in range(4 * Y):
            b, p = i // (2 * Y), i % (2 * Y)
            xx, yy, cc = 2 * c + b, p // 2, p % 2
            src = part.at[pl.ds(b * T + p * PT, PT), :]
            me = (xx == x) & (yy == y) & (cc == c)

            @pl.when(jnp.logical_not(me))
            def _():
                fn_remote(remote(src, red.at[slot], red_send.at[i], red_recv, dev(xx, yy, z, cc)))

            if fn_local is not None:

                @pl.when(me)
                def _():
                    fn_local(pltpu.make_async_copy(src, red.at[slot], red_recv))

    scatter(lambda s: s.start(), lambda s: s.start())
    arrived(red, red_recv)
    pos = 2 * y + c
    acc = red[0]
    for n in range(1, X * Y):
        acc = acc + red[n]
    err[0] = acc

    spread = []
    for d in range(1, 2 * Y):
        p = (pos + d) % (2 * Y)
        spread.append(remote(err.at[0], fin.at[2 * Y - d], fin_send.at[d], fin_recv.at[d], dev(x, p // 2, z, p % 2)))
    for s in spread:
        s.start()
    fin[0] = acc
    for s in spread:
        s.wait()
    sums = jnp.concatenate([fin[(n + 2 * Y - pos) % (2 * Y)] for n in range(2 * Y)], axis=0).T
    x0_real = noisy_wide - sigma * (baseT + sums[:C])
    x0_fake = noisy_wide - sigma * (baseT + sums[C:])
    gap = jnp.abs(lat_ref[...].astype(F32) - x0_real)
    err[1, 0:8] = jnp.sum(gap.reshape(C // 8, 8, T), axis=0)
    errs[0] = err[1, 0:8]
    S = X * Z
    tell = []
    for d in range(1, S):
        where = {"group": group, "seq": (seq + d) % S, "head": hd}
        tell.append(remote(err.at[1, pl.ds(0, 8)], errs.at[d], err_send.at[d], err_recv.at[d], where))
    for s in tell:
        s.start()
    for s in tell:
        s.wait()
    tot = errs[0]
    for n in range(1, S):
        tot = tot + errs[n]
    tot = jnp.sum(jnp.sum(tot, axis=0, keepdims=True), axis=1, keepdims=True)
    weight = tot / (T * S * C)
    out_ref[...] = (x0_fake - x0_real) / weight

    for i in range(2):
        j = 2 * c + i
        for n, (src, dst) in enumerate(exchange(i)):

            @pl.when(j != x)
            def _():
                remote(src, dst, xs_send.at[i, n], xs_recv.at[xslot, n], dev(j, y, z, x // 2)).wait_send()

    give.wait_send()
    for s in sends + wring + kring + cross:
        s.wait_send()
    scatter(lambda s: s.wait_send(), None)


def local(
    latents, noise, step, stream, patch_embed_weight, prenorm_gain_vector, query_matrix,
    key_matrix, value_matrix, output_matrix, velocity_readout_weight, adapter_query_down,
    adapter_query_up, adapter_output_down, adapter_output_up, *, dims,
):
    Y, Z, YL = dims
    T, D = stream.shape
    C = latents.shape[1]
    R = query_matrix.shape[0]
    PT = T // (2 * Y)
    H = Z // 2
    vmem = pl.BlockSpec(memory_space=pltpu.VMEM)
    hbm = pl.BlockSpec(memory_space=pl.ANY)
    dma = pltpu.SemaphoreType.DMA
    out = pl.pallas_call(
        functools.partial(kernel, dims),
        out_shape=jax.ShapeDtypeStruct((C, T), F32),
        in_specs=[pl.BlockSpec(memory_space=pltpu.SMEM), vmem, vmem, hbm, hbm] + [vmem] * 5 + [hbm] + [vmem] * 3 + [hbm],
        out_specs=vmem,
        scratch_shapes=[
            pltpu.VMEM((T, D), BF16),
            pltpu.VMEM((C, D), BF16),
            pltpu.VMEM((C, D), BF16),
            pltpu.VMEM((HEAD, D), BF16),
            pltpu.VMEM((T, D), BF16),
            pltpu.VMEM((X, T, D // 2), BF16),
            pltpu.VMEM((2, Z * R, 3 * HEAD), BF16),
            pltpu.VMEM((Z, 64 + C, HEAD), BF16),
            pltpu.VMEM((2, Z * R, HEAD), BF16),
            pltpu.VMEM((32, HEAD), BF16),
            pltpu.VMEM((2, C, HEAD), F32),
            pltpu.VMEM((2, C, HEAD), F32),
            pltpu.VMEM((2, HEAD, 2 * HEAD), BF16),
            pltpu.VMEM((2, 2 * HEAD, HEAD), BF16),
            pltpu.VMEM((X * T, 2 * HEAD), F32),
            pltpu.VMEM((2 * T, 2 * HEAD), F32),
            pltpu.VMEM((X * T, 2 * HEAD), F32),
            pltpu.VMEM((2 * T, 2 * HEAD), F32),
            pltpu.VMEM((C, HEAD), F32),
            pltpu.VMEM((C, HEAD), F32),
            pltpu.VMEM((HEAD, 2 * T), BF16),
            pltpu.VMEM((2, Z, 2 * T, 2 * HEAD), BF16),
            pltpu.VMEM((4 * T, HEAD), BF16),
            pltpu.VMEM((4 * T, HEAD), F32),
            pltpu.VMEM((4 * T, HEAD), F32),
            pltpu.VMEM((4 * T, HEAD), F32),
            pltpu.VMEM((2 * T, 2 * C), F32),
            pltpu.VMEM((X * Y, PT, 2 * C), F32),
            pltpu.VMEM((2 * Y, PT, 2 * C), F32),
            pltpu.VMEM((2, PT, 2 * C), F32),
            pltpu.VMEM((X * Z, 8, 2 * C), F32),
            dma((4,)),
            dma((2, 5)), dma((2, 5)),
            dma((X,)), dma((X,)),
            dma((Y,)), dma((Y,)),
            dma((2, H, SUBS)), dma((2, H, SUBS)),
            dma((2, H)), dma((2, H)),
            dma((5,)), dma((5,)),
            dma((Y,)), dma((Y,)),
            dma((2, H, SUBS)), dma((2, H, SUBS)),
            dma((Z,)), dma((Z,)),
            dma((4 * Y,)), dma,
            dma((2 * Y,)), dma((2 * Y,)),
            dma((X * Z,)), dma((X * Z,)),
        ],
        compiler_params=pltpu.CompilerParams(
            collective_id=0, has_side_effects=True, vmem_limit_bytes=56 * 1024 * 1024
        ),
    )(
        step, latents.T, noise.T, stream, patch_embed_weight, prenorm_gain_vector.reshape(1, D),
        query_matrix, key_matrix, value_matrix, output_matrix.T, velocity_readout_weight,
        adapter_query_down, adapter_query_up, adapter_output_down, adapter_output_up,
    )
    return out.T


def solution(mesh):
    heads = ("group", "head")
    in_specs = (
        P("seq", None), P("seq", None), P(), P("seq", None), P(), P(),
        P("seq", heads), P("seq", heads), P("seq", heads), P(heads, "seq"),
        P(), P("seq", None), P(None, heads), P(heads, None), P(),
    )
    YL = mesh.shape["head"] // 2
    dims = (mesh.shape["group"] * YL, mesh.shape["seq"] // X, YL)
    return jax.shard_map(
        functools.partial(local, dims=dims), mesh=mesh, in_specs=in_specs,
        out_specs=P("seq", None), check_vma=False,
    )
```

```python
import functools

import jax
import jax.numpy as jnp
from jax import lax
from jax.experimental import pallas as pl
from jax.experimental.pallas import tpu as pltpu
from jax.sharding import PartitionSpec as P

HEAD = 128
X = 4
MESH = pl.DeviceIdType.MESH
BF16 = jnp.bfloat16
F32 = jnp.float32


def dot_t(left, right):
    return lax.dot_general(
        left, right, (((1,), (1,)), ((), ())), preferred_element_type=F32
    )


def dot(left, right):
    return jnp.dot(left, right, preferred_element_type=F32)


WPARTS = 2
KPARTS = 2


def kernel(
    dims,
    step_ref,
    lat_ref,
    noise_ref,
    stream_hbm,
    pe_hbm,
    gain_ref,
    wq_ref,
    wk_ref,
    wv_ref,
    om_ref,
    vel_hbm,
    ad_ref,
    aup_ref,
    aod_ref,
    aou_hbm,
    out_ref,
    stream_ref,
    pe_ref,
    vel_ref,
    aou_ref,
    hid,
    acts,
    wkv,
    wqb,
    ext,
    wlow,
    lpack,
    mpart,
    mpair,
    aup_all,
    aod_all,
    pacc,
    precv,
    qacc,
    qrecv,
    mhalf,
    mrecv,
    loraT,
    kv,
    q2,
    top_ref,
    sum_ref,
    acc_ref,
    part,
    red,
    fin,
    err,
    errs,
    load_sem,
    xs_send,
    xs_recv,
    a_send,
    a_recv,
    ay_send,
    ay_recv,
    wr_send,
    wr_recv,
    wq_send,
    wq_recv,
    we_send,
    we_recv,
    d_send,
    d_recv,
    lo_send,
    lo_recv,
    kr_send,
    kr_recv,
    kd_send,
    kd_recv,
    red_send,
    red_recv,
    fin_send,
    fin_recv,
    err_send,
    err_recv,
):
    Y, Z, YL = dims
    T, D = stream_ref.shape
    half = D // 2
    R = wq_ref.shape[0]
    C = lat_ref.shape[0]
    PT = T // (2 * Y)
    H = Z // 2
    G = R // 32
    LC = 16
    group = lax.axis_index("group")
    seq = lax.axis_index("seq")
    hd = lax.axis_index("head")
    y = group * YL + hd // 2
    c = hd % 2
    x = seq // Z
    z = seq % Z
    o = 1 - c

    def dev(xx, yy, zz, cc):
        return {"group": yy // YL, "seq": xx * Z + zz, "head": (yy % YL) * 2 + cc}

    def remote(src, dst, ssem, rsem, where):
        return pltpu.make_async_remote_copy(
            src_ref=src, dst_ref=dst, send_sem=ssem, recv_sem=rsem,
            device_id=where, device_id_type=MESH,
        )

    def arrived(ref, sem):
        pltpu.make_async_copy(ref, ref, sem).wait()

    loads = [
        pltpu.make_async_copy(src, dst, load_sem.at[n])
        for n, (src, dst) in enumerate(
            ((vel_hbm, vel_ref), (stream_hbm, stream_ref), (pe_hbm, pe_ref), (aou_hbm, aou_ref))
        )
    ]
    for l in loads:
        l.start()

    if LC * Y < HEAD:
        loraT[...] = jnp.zeros(loraT.shape, BF16)

    barrier = pltpu.get_barrier_semaphore()
    line = [dev(x, y, z, o)]
    for d in range(1, X):
        line += [dev((x + d) % X, y, z, c), dev((x + d) % X, y, z, o)]
    for d in range(1, Y):
        line += [dev(x, (y + d) % Y, z, c), dev(x, (y + d) % Y, z, o)]
    for d in range(1, Z):
        line.append(dev(x, y, (z + d) % Z, c))
    for where in line:
        pl.semaphore_signal(barrier, inc=1, device_id=where, device_id_type=MESH)

    loads[0].wait()
    lo = R * seq // 128
    window = vel_ref[:, pl.ds(pl.multiple_of(lo * 128, 128), 256)].astype(F32)
    off = R * seq - lo * 128
    turned = pltpu.roll(window, lax.rem(256 - off, 256), 1).astype(BF16)
    mp = dot(turned[:, :R], om_ref[...])
    mpart[0] = mp[:, :HEAD]
    mpart[1] = mp[:, HEAD:]

    low = pltpu.roll(ad_ref[...].astype(F32), lax.rem(128 - LC * y, 128), 1)
    lane = lax.broadcasted_iota(jnp.int32, (32, 128), 1)
    packed = jnp.zeros((32, 128), F32)
    for g in range(G):
        turned_low = low[32 * g : 32 * (g + 1)]
        if g:
            turned_low = pltpu.roll(turned_low, LC * g, 1)
        packed = jnp.where((lane >= LC * g) & (lane < LC * (g + 1)), turned_low, packed)
    lpack[...] = packed.astype(BF16)

    pl.semaphore_wait(barrier, len(line))

    xslot = x % 2
    myrows = pl.ds(pl.multiple_of(R * z, 16), R)

    def exchange(i):
        mine_ = pl.ds(HEAD * i, HEAD)
        return [
            (wk_ref.at[:, mine_], wkv.at[xslot, myrows, pl.ds(0, HEAD)]),
            (wv_ref.at[:, mine_], wkv.at[xslot, myrows, pl.ds(HEAD, HEAD)]),
            (wq_ref.at[:, mine_], wqb.at[xslot, myrows, :]),
            (lpack, ext.at[z, pl.ds(pl.multiple_of(32 * xslot, 16), 32), :]),
            (mpart.at[i], mpair.at[xslot]),
        ]

    for i in range(2):
        j = 2 * c + i
        for n, (src, dst) in enumerate(exchange(i)):

            @pl.when(j != x)
            def _():
                remote(src, dst, xs_send.at[i, n], xs_recv.at[xslot, n], dev(j, y, z, x // 2)).start()

            @pl.when(j == x)
            def _():
                pltpu.make_async_copy(src, dst, xs_recv.at[xslot, n]).start()

    other = dev(x, y, z, o)
    up = remote(aup_ref, aup_all.at[c], d_send.at[0], d_recv.at[0], other)
    od = remote(aod_ref, aod_all.at[c], d_send.at[1], d_recv.at[1], other)
    up.start()
    od.start()
    aup_all[c] = aup_ref[...]
    aod_all[c] = aod_ref[...]

    level = (jnp.full((1, 1), step_ref[0], jnp.int32).astype(F32) + 1.0) / 1000.0
    sigma = 5.0 * level / (1.0 + 4.0 * level)
    noisyT = ((1.0 - sigma) * lat_ref[...].astype(F32) + sigma * noise_ref[...].astype(F32)).astype(BF16)
    noisy_wide = noisyT.astype(F32)
    noisy = noisy_wide.T.astype(BF16)
    loads[1].wait()
    loads[2].wait()
    wide = 640 if D % 640 == 0 else D
    total = jnp.zeros((T, 1), F32)
    for k in range(D // wide):
        cols = slice(k * wide, (k + 1) * wide)
        h = (stream_ref[:, cols].astype(F32) + dot(noisy, pe_ref[:, cols])).astype(BF16)
        hid[:, cols] = h
        hw = h.astype(F32)
        total = total + jnp.sum(hw * hw, axis=1, keepdims=True)
    scale = lax.rsqrt(total / D + 1e-06)
    for k in range(half // wide):
        at = pl.ds(pl.multiple_of(c * half + k * wide, 128), wide)
        n = (hid[:, at].astype(F32) * scale * gain_ref[:, at]).astype(BF16)
        acts[x, :, k * wide : (k + 1) * wide] = n

    YT = T // Y
    Q4 = half // 4
    xo, xr, xl = (x + 2) % X, (x + 1) % X, (x + 3) % X

    def yrows(block, yy):
        return acts.at[block, pl.ds(pl.multiple_of(YT * yy, 16), YT), pl.ds(0, 2 * Q4)]

    def acols(block, lo_, n):
        return acts.at[block, :, pl.ds(lo_ * Q4, n * Q4)]

    sends = []

    def send_acts(ref, n, where):
        s = remote(ref, ref, a_send.at[n], a_recv.at[n], dev(where, y, z, c))
        s.start()
        sends.append(s)

    send_acts(yrows(x, y), 0, xo)
    send_acts(acols(x, 2, 1), 1, xr)
    send_acts(acols(x, 3, 1), 2, xl)
    send_acts(acols(x, 0, 2), 3, xr)
    send_acts(acols(x, 3, 1), 4, xr)
    send_acts(acols(x, 0, 3), 5, xl)

    right, left = dev(x, y, (z + 1) % Z, c), dev(x, y, (z + Z - 1) % Z, c)

    def ring(piece, parts, ssem, rsem, t, extra=None):
        turns = [
            (piece(((z + Z - t) % Z, (z + t) % Z)[way], n), way, ssem.at[way, t, n], rsem.at[way, t, n],
             rsem.at[way, t - 1, n] if t else None, t < H - 1 or n // (parts // 2) == way)
            for n in range(parts)
            for way in range(2)
        ]
        if extra is not None:
            ebox, es, er = extra
            turns[2:2] = [
                (ebox(((z + Z - t) % Z, (z + t) % Z)[way], 0), way, es.at[way, t], er.at[way, t],
                 er.at[way, t - 1] if t else None, t < H - 1 or way == 0)
                for way in range(2)
            ]
        started = []
        for ref, way, ss, rs, before, goes in turns:
            if goes:
                if t:
                    arrived(ref, before)
                s = remote(ref, ref, ss, rs, (right, left)[way])
                s.start()
                started.append(s)
        for ref, way, ss, rs, before, goes in turns:
            if t and not goes:
                arrived(ref, before)
        return started

    def last(piece, parts, rsem, extra=None):
        zz = (z + H) % Z
        for n in range(parts):
            arrived(piece(zz, n), rsem.at[n // (parts // 2), H - 1, n])
        if extra is not None:
            arrived(extra[0](zz, 0), extra[2].at[0, H - 1])

    def wpiece(zz, n):
        return wkv.at[n, pl.ds(pl.multiple_of(R * zz, 16), R), :]

    def qpiece(zz, n):
        return wqb.at[n, pl.ds(pl.multiple_of(R * zz, 16), R), :]

    def epiece(zz, n):
        return ext.at[zz]

    side = (epiece, we_send, we_recv)
    wring = []

    def ring1(t):
        wring.extend(ring(wpiece, WPARTS, wr_send, wr_recv, t))

    def ring2(t):
        wring.extend(ring(qpiece, 2, wq_send, wq_recv, t, side))

    def unpack(zz):
        for s in range(2):
            piece = ext[zz, 32 * s : 32 * (s + 1)].astype(F32)
            for g in range(G):
                rows = pltpu.roll(piece, 128 - LC * g, 1) if g else piece
                wlow[s, pl.ds(pl.multiple_of(R * zz + 32 * g, 16), 32), :] = rows.astype(BF16)
        mhalf[...] += ext[zz, 64 : 64 + C].astype(F32)

    for s in range(2):
        for n in range(2):
            arrived(wkv.at[s, myrows, pl.ds(HEAD * n, HEAD)], xs_recv.at[s, n])
    ring1(0)
    for s in range(2):
        arrived(wqb.at[s, myrows, :], xs_recv.at[s, 2])
        arrived(ext.at[z, pl.ds(32 * s, 32), :], xs_recv.at[s, 3])
        arrived(mpair.at[s], xs_recv.at[s, 4])
    ext[z, 64 : 64 + C] = (mpair[0] + mpair[1]).astype(BF16)

    ring2(0)
    arrived(yrows(xo, y), a_recv.at[0])
    for d in range(1, Y):
        s = remote(yrows(xo, y), yrows(xo, y), ay_send.at[d], ay_recv.at[d], dev(x, (y + d) % Y, z, c))
        s.start()
        sends.append(s)
    if H > 1:
        ring1(1)
    arrived(acols(xl, 2, 1), a_recv.at[1])
    send_acts(acols(xl, 2, 1), 6, xr)
    arrived(acols(xr, 3, 1), a_recv.at[2])
    send_acts(acols(xr, 3, 1), 7, xl)
    if H > 1:
        ring2(1)
    baseT = dot_t(vel_ref[...], hid[...])
    mhalf[...] = jnp.zeros(mhalf.shape, F32)
    unpack(z)
    if H > 1:
        unpack((z + Z - 1) % Z)
        unpack((z + 1) % Z)
    loads[3].wait()
    readout = dot_t(vel_ref[...], aou_ref[...]).astype(BF16)
    for t in range(2, H):
        ring1(t)
        ring2(t)
        unpack((z + Z - t) % Z)
        unpack((z + t) % Z)
    last(wpiece, WPARTS, wr_recv)
    last(qpiece, 2, wq_recv, side)
    arrived(acols(xl, 0, 2), a_recv.at[3])
    arrived(acols(xl, 3, 1), a_recv.at[4])
    arrived(acols(xr, 0, 3), a_recv.at[5])
    arrived(acols(xo, 2, 1), a_recv.at[6])
    arrived(acols(xo, 3, 1), a_recv.at[7])
    for d in range(1, Y):
        arrived(yrows(xo, y), ay_recv.at[d])

    ZR = Z * R
    theirs = pl.ds(pl.multiple_of(2 * T * o, 16), 2 * T)
    mine = pl.ds(pl.multiple_of(2 * T * c, 16), 2 * T)
    for b in range(X):
        pacc[b * T : (b + 1) * T] = dot(acts[b, :, :ZR], wkv[0]) + dot(acts[b, :, ZR:], wkv[1])
    give = remote(pacc.at[theirs], precv, d_send.at[2], d_recv.at[2], other)
    give.start()

    give.wait_recv()
    kv[c, z] = (pacc[mine] + precv[...]).astype(BF16)

    def kpiece(zz, n):
        return kv.at[c, zz, pl.ds(n * (2 * T // KPARTS), 2 * T // KPARTS), :]

    def across(zz):
        s = remote(kv.at[c, zz], kv.at[c, zz], kd_send.at[zz], kd_recv.at[zz], other)
        s.start()
        return s

    kring = []
    cross = []

    def ring3(t):
        kring.extend(ring(kpiece, KPARTS, kr_send, kr_recv, t))
        cross.append(across((z + Z - t) % Z))
        if t:
            cross.append(across((z + t) % Z))

    ring3(0)
    unpack((z + H) % Z)
    givem = remote(mhalf, mrecv, d_send.at[3], d_recv.at[3], other)
    givem.start()

    for b in range(X):
        qacc[b * T : (b + 1) * T, :HEAD] = dot(acts[b, :, :ZR], wqb[0]) + dot(acts[b, :, ZR:], wqb[1])
        qacc[b * T : (b + 1) * T, HEAD:] = dot(acts[b, :, :ZR], wlow[0]) + dot(acts[b, :, ZR:], wlow[1])
    giveq = remote(qacc.at[theirs], qrecv, d_send.at[4], d_recv.at[4], other)
    giveq.start()
    if H > 1:
        ring3(1)
    up.wait()
    od.wait()
    givem.wait()
    mixw = mhalf[...] + mrecv[...]
    mix = mixw.astype(BF16)
    at = pl.ds(pl.multiple_of(HEAD * (x % 2), HEAD), HEAD)
    fmix = (mixw + dot_t(readout, aod_all[x // 2, at, :])).astype(BF16)
    zero = jnp.zeros_like(mix)
    mix = jnp.concatenate([mix, zero], axis=0)
    fmix = jnp.concatenate([zero, fmix], axis=0)
    giveq.wait()
    qsum = qacc[mine] + qrecv[...]
    lrows = pl.ds(pl.multiple_of(LC * y, 16), LC)
    loraT[lrows, :] = qsum[:, HEAD:].T[:LC].astype(BF16)
    for d in range(1, Y):
        s = remote(loraT.at[lrows], loraT.at[lrows], lo_send.at[d], lo_recv.at[d], dev(x, (y + d) % Y, z, c))
        s.start()
        sends.append(s)
    logit = HEAD ** (-0.5)
    q2[: 2 * T] = (qsum[:, :HEAD] * logit).astype(BF16)
    top_ref[...] = jnp.full(top_ref.shape, -jnp.inf, F32)
    sum_ref[...] = jnp.zeros(sum_ref.shape, F32)
    acc_ref[...] = jnp.zeros(acc_ref.shape, F32)

    def attend(cc, zz):
        for st in range(2):
            rows = slice(2 * T * st, 2 * T * (st + 1))
            s = dot_t(q2[rows], kv[cc, zz, :, :HEAD])
            best = s[:, :HEAD]
            for g in range(1, 2 * T // HEAD):
                best = jnp.maximum(best, s[:, g * HEAD : (g + 1) * HEAD])
            old = top_ref[rows]
            new = jnp.maximum(old, jnp.max(best, axis=1, keepdims=True))
            fade = jnp.exp(old - new)
            ps = [jnp.exp(s[:, g * HEAD : (g + 1) * HEAD] - new) for g in range(2 * T // HEAD)]
            l = sum_ref[rows] * fade
            for p in ps:
                l = l + p
            sum_ref[rows] = l
            top_ref[rows] = new
            probs = jnp.concatenate([p.astype(BF16) for p in ps], axis=1)
            acc_ref[rows] = acc_ref[rows] * fade + dot(probs, kv[cc, zz, :, HEAD:])

    def attend_both(zz):
        attend(c, zz)
        arrived(kv.at[o, zz], kd_recv.at[zz])
        attend(o, zz)

    for t in range(1, H):
        if t > 1:
            ring3(t)
        if t == min(2, H - 1):
            for d in range(1, Y):
                arrived(loraT.at[lrows], lo_recv.at[d])
            delta = lax.dot_general(
                loraT[...], aup_all[x // 2, :, at], (((0,), (0,)), ((), ())), preferred_element_type=F32
            )
            q2[2 * T :] = ((qsum[:, :HEAD] + delta) * logit).astype(BF16)
            attend_both(z)
        if t > 1:
            attend_both((z + Z - t + 1) % Z)
            attend_both((z + t - 1) % Z)
    if H == 1:
        for d in range(1, Y):
            arrived(loraT.at[lrows], lo_recv.at[d])
        delta = lax.dot_general(
            loraT[...], aup_all[x // 2, :, at], (((0,), (0,)), ((), ())), preferred_element_type=F32
        )
        q2[2 * T :] = ((qsum[:, :HEAD] + delta) * logit).astype(BF16)
        attend_both(z)
    else:
        attend_both((z + Z - H + 1) % Z)
        attend_both((z + H - 1) % Z)
    last(kpiece, KPARTS, kr_recv)
    cross.append(across((z + H) % Z))
    attend_both((z + H) % Z)

    attn = (acc_ref[...] / jnp.sum(sum_ref[...], axis=1, keepdims=True)).astype(BF16)
    part[...] = dot_t(attn[: 2 * T], mix) + dot_t(attn[2 * T :], fmix)

    slot = x * Y + y

    def scatter(fn_remote, fn_local):
        for i in range(4 * Y):
            b, p = i // (2 * Y), i % (2 * Y)
            xx, yy, cc = 2 * c + b, p // 2, p % 2
            src = part.at[pl.ds(b * T + p * PT, PT), :]
            me = (xx == x) & (yy == y) & (cc == c)

            @pl.when(jnp.logical_not(me))
            def _():
                fn_remote(remote(src, red.at[slot], red_send.at[i], red_recv, dev(xx, yy, z, cc)))

            if fn_local is not None:

                @pl.when(me)
                def _():
                    fn_local(pltpu.make_async_copy(src, red.at[slot], red_recv))

    scatter(lambda s: s.start(), lambda s: s.start())
    arrived(red, red_recv)
    pos = 2 * y + c
    acc = red[0]
    for n in range(1, X * Y):
        acc = acc + red[n]
    err[0] = acc

    spread = []
    for d in range(1, 2 * Y):
        p = (pos + d) % (2 * Y)
        spread.append(remote(err.at[0], fin.at[2 * Y - d], fin_send.at[d], fin_recv.at[d], dev(x, p // 2, z, p % 2)))
    for s in spread:
        s.start()
    fin[0] = acc
    for s in spread:
        s.wait()
    sums = jnp.concatenate([fin[(n + 2 * Y - pos) % (2 * Y)] for n in range(2 * Y)], axis=0).T
    x0_real = noisy_wide - sigma * (baseT + sums[:C])
    x0_fake = noisy_wide - sigma * (baseT + sums[C:])
    gap = jnp.abs(lat_ref[...].astype(F32) - x0_real)
    err[1, 0:8] = jnp.sum(gap.reshape(C // 8, 8, T), axis=0)
    errs[0] = err[1, 0:8]
    S = X * Z
    tell = []
    for d in range(1, S):
        where = {"group": group, "seq": (seq + d) % S, "head": hd}
        tell.append(remote(err.at[1, pl.ds(0, 8)], errs.at[d], err_send.at[d], err_recv.at[d], where))
    for s in tell:
        s.start()
    for s in tell:
        s.wait()
    tot = errs[0]
    for n in range(1, S):
        tot = tot + errs[n]
    tot = jnp.sum(jnp.sum(tot, axis=0, keepdims=True), axis=1, keepdims=True)
    weight = tot / (T * S * C)
    out_ref[...] = (x0_fake - x0_real) / weight

    for i in range(2):
        j = 2 * c + i
        for n, (src, dst) in enumerate(exchange(i)):

            @pl.when(j != x)
            def _():
                remote(src, dst, xs_send.at[i, n], xs_recv.at[xslot, n], dev(j, y, z, x // 2)).wait_send()

    give.wait_send()
    for s in sends + wring + kring + cross:
        s.wait_send()
    scatter(lambda s: s.wait_send(), None)


def local(
    latents, noise, step, stream, patch_embed_weight, prenorm_gain_vector, query_matrix,
    key_matrix, value_matrix, output_matrix, velocity_readout_weight, adapter_query_down,
    adapter_query_up, adapter_output_down, adapter_output_up, *, dims,
):
    Y, Z, YL = dims
    T, D = stream.shape
    C = latents.shape[1]
    R = query_matrix.shape[0]
    PT = T // (2 * Y)
    H = Z // 2
    vmem = pl.BlockSpec(memory_space=pltpu.VMEM)
    hbm = pl.BlockSpec(memory_space=pl.ANY)
    dma = pltpu.SemaphoreType.DMA
    out = pl.pallas_call(
        functools.partial(kernel, dims),
        out_shape=jax.ShapeDtypeStruct((C, T), F32),
        in_specs=[pl.BlockSpec(memory_space=pltpu.SMEM), vmem, vmem, hbm, hbm] + [vmem] * 5 + [hbm] + [vmem] * 3 + [hbm],
        out_specs=vmem,
        scratch_shapes=[
            pltpu.VMEM((T, D), BF16),
            pltpu.VMEM((C, D), BF16),
            pltpu.VMEM((C, D), BF16),
            pltpu.VMEM((HEAD, D), BF16),
            pltpu.VMEM((T, D), BF16),
            pltpu.VMEM((X, T, D // 2), BF16),
            pltpu.VMEM((2, Z * R, 2 * HEAD), BF16),
            pltpu.VMEM((2, Z * R, HEAD), BF16),
            pltpu.VMEM((Z, 64 + C, HEAD), BF16),
            pltpu.VMEM((2, Z * R, HEAD), BF16),
            pltpu.VMEM((32, HEAD), BF16),
            pltpu.VMEM((2, C, HEAD), F32),
            pltpu.VMEM((2, C, HEAD), F32),
            pltpu.VMEM((2, HEAD, 2 * HEAD), BF16),
            pltpu.VMEM((2, 2 * HEAD, HEAD), BF16),
            pltpu.VMEM((X * T, 2 * HEAD), F32),
            pltpu.VMEM((2 * T, 2 * HEAD), F32),
            pltpu.VMEM((X * T, 2 * HEAD), F32),
            pltpu.VMEM((2 * T, 2 * HEAD), F32),
            pltpu.VMEM((C, HEAD), F32),
            pltpu.VMEM((C, HEAD), F32),
            pltpu.VMEM((HEAD, 2 * T), BF16),
            pltpu.VMEM((2, Z, 2 * T, 2 * HEAD), BF16),
            pltpu.VMEM((4 * T, HEAD), BF16),
            pltpu.VMEM((4 * T, HEAD), F32),
            pltpu.VMEM((4 * T, HEAD), F32),
            pltpu.VMEM((4 * T, HEAD), F32),
            pltpu.VMEM((2 * T, 2 * C), F32),
            pltpu.VMEM((X * Y, PT, 2 * C), F32),
            pltpu.VMEM((2 * Y, PT, 2 * C), F32),
            pltpu.VMEM((2, PT, 2 * C), F32),
            pltpu.VMEM((X * Z, 8, 2 * C), F32),
            dma((4,)),
            dma((2, 5)), dma((2, 5)),
            dma((8,)), dma((8,)),
            dma((Y,)), dma((Y,)),
            dma((2, H, WPARTS)), dma((2, H, WPARTS)),
            dma((2, H, 2)), dma((2, H, 2)),
            dma((2, H)), dma((2, H)),
            dma((5,)), dma((5,)),
            dma((Y,)), dma((Y,)),
            dma((2, H, KPARTS)), dma((2, H, KPARTS)),
            dma((Z,)), dma((Z,)),
            dma((4 * Y,)), dma,
            dma((2 * Y,)), dma((2 * Y,)),
            dma((X * Z,)), dma((X * Z,)),
        ],
        compiler_params=pltpu.CompilerParams(
            collective_id=0, has_side_effects=True, vmem_limit_bytes=56 * 1024 * 1024
        ),
    )(
        step, latents.T, noise.T, stream, patch_embed_weight, prenorm_gain_vector.reshape(1, D),
        query_matrix, key_matrix, value_matrix, output_matrix.T, velocity_readout_weight,
        adapter_query_down, adapter_query_up, adapter_output_down, adapter_output_up,
    )
    return out.T


def solution(mesh):
    heads = ("group", "head")
    in_specs = (
        P("seq", None), P("seq", None), P(), P("seq", None), P(), P(),
        P("seq", heads), P("seq", heads), P("seq", heads), P(heads, "seq"),
        P(), P("seq", None), P(None, heads), P(heads, None), P(),
    )
    YL = mesh.shape["head"] // 2
    dims = (mesh.shape["group"] * YL, mesh.shape["seq"] // X, YL)
    return jax.shard_map(
        functools.partial(local, dims=dims), mesh=mesh, in_specs=in_specs,
        out_specs=P("seq", None), check_vma=False,
    )
```

```python
import functools

import jax
import jax.numpy as jnp
from jax import lax
from jax.experimental import pallas as pl
from jax.experimental.pallas import tpu as pltpu
from jax.sharding import PartitionSpec as P

HEAD = 128
X = 4
MESH = pl.DeviceIdType.MESH
BF16 = jnp.bfloat16
F32 = jnp.float32


def dot_t(left, right):
    return lax.dot_general(
        left, right, (((1,), (1,)), ((), ())), preferred_element_type=F32
    )


def dot(left, right):
    return jnp.dot(left, right, preferred_element_type=F32)


WPARTS = 2
KPARTS = 2


def kernel(
    dims,
    step_ref,
    lat_ref,
    noise_ref,
    stream_hbm,
    pe_hbm,
    gain_ref,
    wq_ref,
    wk_ref,
    wv_ref,
    om_ref,
    vel_hbm,
    ad_ref,
    aup_ref,
    aod_ref,
    aou_hbm,
    out_ref,
    stream_ref,
    pe_ref,
    vel_ref,
    aou_ref,
    hid,
    acts,
    wkv,
    wqb,
    ext,
    wlow,
    lpack,
    mpart,
    mpair,
    aup_all,
    aod_all,
    pacc,
    precv,
    qacc,
    qrecv,
    mhalf,
    mrecv,
    loraT,
    kv,
    q2,
    top_ref,
    sum_ref,
    acc_ref,
    part,
    red,
    fin,
    err,
    errs,
    load_sem,
    xs_send,
    xs_recv,
    a_send,
    a_recv,
    ay_send,
    ay_recv,
    wr_send,
    wr_recv,
    wq_send,
    wq_recv,
    we_send,
    we_recv,
    d_send,
    d_recv,
    lo_send,
    lo_recv,
    kr_send,
    kr_recv,
    kd_send,
    kd_recv,
    red_send,
    red_recv,
    own_send,
    fin_send,
    fin_recv,
    err_send,
    err_recv,
):
    Y, Z, YL = dims
    T, D = stream_ref.shape
    half = D // 2
    R = wq_ref.shape[0]
    C = lat_ref.shape[0]
    PT = T // (2 * Y)
    H = Z // 2
    G = R // 32
    LC = 16
    group = lax.axis_index("group")
    seq = lax.axis_index("seq")
    hd = lax.axis_index("head")
    y = group * YL + hd // 2
    c = hd % 2
    x = seq // Z
    z = seq % Z
    o = 1 - c

    def dev(xx, yy, zz, cc):
        return {"group": yy // YL, "seq": xx * Z + zz, "head": (yy % YL) * 2 + cc}

    def remote(src, dst, ssem, rsem, where):
        return pltpu.make_async_remote_copy(
            src_ref=src, dst_ref=dst, send_sem=ssem, recv_sem=rsem,
            device_id=where, device_id_type=MESH,
        )

    def arrived(ref, sem):
        pltpu.make_async_copy(ref, ref, sem).wait()

    loads = [
        pltpu.make_async_copy(src, dst, load_sem.at[n])
        for n, (src, dst) in enumerate(
            ((vel_hbm, vel_ref), (stream_hbm, stream_ref), (pe_hbm, pe_ref), (aou_hbm, aou_ref))
        )
    ]
    for l in loads:
        l.start()

    if LC * Y < HEAD:
        loraT[...] = jnp.zeros(loraT.shape, BF16)

    barrier = pltpu.get_barrier_semaphore()
    line = [dev(x, y, z, o)]
    for d in range(1, X):
        line += [dev((x + d) % X, y, z, c), dev((x + d) % X, y, z, o)]
    for d in range(1, Y):
        line += [dev(x, (y + d) % Y, z, c), dev(x, (y + d) % Y, z, o)]
    for d in range(1, Z):
        line.append(dev(x, y, (z + d) % Z, c))
    for where in line:
        pl.semaphore_signal(barrier, inc=1, device_id=where, device_id_type=MESH)

    loads[0].wait()
    lo = R * seq // 128
    window = vel_ref[:, pl.ds(pl.multiple_of(lo * 128, 128), 256)].astype(F32)
    off = R * seq - lo * 128
    turned = pltpu.roll(window, lax.rem(256 - off, 256), 1).astype(BF16)
    mp = dot(turned[:, :R], om_ref[...])
    mpart[0] = mp[:, :HEAD]
    mpart[1] = mp[:, HEAD:]

    low = pltpu.roll(ad_ref[...].astype(F32), lax.rem(128 - LC * y, 128), 1)
    lane = lax.broadcasted_iota(jnp.int32, (32, 128), 1)
    packed = jnp.zeros((32, 128), F32)
    for g in range(G):
        turned_low = low[32 * g : 32 * (g + 1)]
        if g:
            turned_low = pltpu.roll(turned_low, LC * g, 1)
        packed = jnp.where((lane >= LC * g) & (lane < LC * (g + 1)), turned_low, packed)
    lpack[...] = packed.astype(BF16)

    pl.semaphore_wait(barrier, len(line))

    xslot = x % 2
    myrows = pl.ds(pl.multiple_of(R * z, 16), R)

    def exchange(i):
        mine_ = pl.ds(HEAD * i, HEAD)
        return [
            (wk_ref.at[:, mine_], wkv.at[xslot, myrows, pl.ds(0, HEAD)]),
            (wv_ref.at[:, mine_], wkv.at[xslot, myrows, pl.ds(HEAD, HEAD)]),
            (wq_ref.at[:, mine_], wqb.at[xslot, myrows, :]),
            (lpack, ext.at[z, pl.ds(pl.multiple_of(32 * xslot, 16), 32), :]),
            (mpart.at[i], mpair.at[xslot]),
        ]

    for i in range(2):
        j = 2 * c + i
        for n, (src, dst) in enumerate(exchange(i)):

            @pl.when(j != x)
            def _():
                remote(src, dst, xs_send.at[i, n], xs_recv.at[xslot, n], dev(j, y, z, x // 2)).start()

            @pl.when(j == x)
            def _():
                pltpu.make_async_copy(src, dst, xs_recv.at[xslot, n]).start()

    other = dev(x, y, z, o)
    up = remote(aup_ref, aup_all.at[c], d_send.at[0], d_recv.at[0], other)
    od = remote(aod_ref, aod_all.at[c], d_send.at[1], d_recv.at[1], other)
    up.start()
    od.start()
    aup_all[c] = aup_ref[...]
    aod_all[c] = aod_ref[...]

    level = (jnp.full((1, 1), step_ref[0], jnp.int32).astype(F32) + 1.0) / 1000.0
    sigma = 5.0 * level / (1.0 + 4.0 * level)
    noisyT = ((1.0 - sigma) * lat_ref[...].astype(F32) + sigma * noise_ref[...].astype(F32)).astype(BF16)
    noisy_wide = noisyT.astype(F32)
    noisy = noisy_wide.T.astype(BF16)
    loads[1].wait()
    loads[2].wait()
    wide = 640 if D % 640 == 0 else D
    total = jnp.zeros((T, 1), F32)
    for k in range(D // wide):
        cols = slice(k * wide, (k + 1) * wide)
        h = (stream_ref[:, cols].astype(F32) + dot(noisy, pe_ref[:, cols])).astype(BF16)
        hid[:, cols] = h
        hw = h.astype(F32)
        total = total + jnp.sum(hw * hw, axis=1, keepdims=True)
    scale = lax.rsqrt(total / D + 1e-06)
    for k in range(half // wide):
        at = pl.ds(pl.multiple_of(c * half + k * wide, 128), wide)
        n = (hid[:, at].astype(F32) * scale * gain_ref[:, at]).astype(BF16)
        acts[x, :, k * wide : (k + 1) * wide] = n

    YT = T // Y
    Q4 = half // 4
    xo, xr, xl = (x + 2) % X, (x + 1) % X, (x + 3) % X

    def yrows(block, yy):
        return acts.at[block, pl.ds(pl.multiple_of(YT * yy, 16), YT), pl.ds(0, 2 * Q4)]

    def acols(block, lo_, n):
        return acts.at[block, :, pl.ds(lo_ * Q4, n * Q4)]

    sends = []

    def send_acts(ref, n, where):
        s = remote(ref, ref, a_send.at[n], a_recv.at[n], dev(where, y, z, c))
        s.start()
        sends.append(s)

    send_acts(yrows(x, y), 0, xo)
    send_acts(acols(x, 2, 1), 1, xr)
    send_acts(acols(x, 3, 1), 2, xl)
    send_acts(acols(x, 0, 2), 3, xr)
    send_acts(acols(x, 3, 1), 4, xr)
    send_acts(acols(x, 0, 3), 5, xl)

    right, left = dev(x, y, (z + 1) % Z, c), dev(x, y, (z + Z - 1) % Z, c)

    def ring(piece, parts, ssem, rsem, t, extra=None):
        turns = [
            (piece(((z + Z - t) % Z, (z + t) % Z)[way], n), way, ssem.at[way, t, n], rsem.at[way, t, n],
             rsem.at[way, t - 1, n] if t else None, t < H - 1 or n // (parts // 2) == way)
            for n in range(parts)
            for way in range(2)
        ]
        if extra is not None:
            ebox, es, er = extra
            turns[2:2] = [
                (ebox(((z + Z - t) % Z, (z + t) % Z)[way], 0), way, es.at[way, t], er.at[way, t],
                 er.at[way, t - 1] if t else None, t < H - 1 or way == 0)
                for way in range(2)
            ]
        started = []
        for ref, way, ss, rs, before, goes in turns:
            if goes:
                if t:
                    arrived(ref, before)
                s = remote(ref, ref, ss, rs, (right, left)[way])
                s.start()
                started.append(s)
        for ref, way, ss, rs, before, goes in turns:
            if t and not goes:
                arrived(ref, before)
        return started

    def last(piece, parts, rsem, extra=None):
        zz = (z + H) % Z
        for n in range(parts):
            arrived(piece(zz, n), rsem.at[n // (parts // 2), H - 1, n])
        if extra is not None:
            arrived(extra[0](zz, 0), extra[2].at[0, H - 1])

    def wpiece(zz, n):
        return wkv.at[n, pl.ds(pl.multiple_of(R * zz, 16), R), :]

    def qpiece(zz, n):
        return wqb.at[n, pl.ds(pl.multiple_of(R * zz, 16), R), :]

    def epiece(zz, n):
        return ext.at[zz]

    side = (epiece, we_send, we_recv)
    wring = []

    def ring1(t):
        wring.extend(ring(wpiece, WPARTS, wr_send, wr_recv, t))

    def ring2(t):
        wring.extend(ring(qpiece, 2, wq_send, wq_recv, t, side))

    def unpack(zz):
        for s in range(2):
            piece = ext[zz, 32 * s : 32 * (s + 1)].astype(F32)
            for g in range(G):
                rows = pltpu.roll(piece, 128 - LC * g, 1) if g else piece
                wlow[s, pl.ds(pl.multiple_of(R * zz + 32 * g, 16), 32), :] = rows.astype(BF16)
        mhalf[...] += ext[zz, 64 : 64 + C].astype(F32)

    for s in range(2):
        for n in range(2):
            arrived(wkv.at[s, myrows, pl.ds(HEAD * n, HEAD)], xs_recv.at[s, n])
    ring1(0)
    for s in range(2):
        arrived(wqb.at[s, myrows, :], xs_recv.at[s, 2])
        arrived(ext.at[z, pl.ds(32 * s, 32), :], xs_recv.at[s, 3])
        arrived(mpair.at[s], xs_recv.at[s, 4])
    ext[z, 64 : 64 + C] = (mpair[0] + mpair[1]).astype(BF16)

    ring2(0)
    arrived(yrows(xo, y), a_recv.at[0])
    for d in range(1, Y):
        s = remote(yrows(xo, y), yrows(xo, y), ay_send.at[d], ay_recv.at[d], dev(x, (y + d) % Y, z, c))
        s.start()
        sends.append(s)
    if H > 1:
        ring1(1)
    arrived(acols(xl, 2, 1), a_recv.at[1])
    send_acts(acols(xl, 2, 1), 6, xr)
    arrived(acols(xr, 3, 1), a_recv.at[2])
    send_acts(acols(xr, 3, 1), 7, xl)
    if H > 1:
        ring2(1)
    baseT = dot_t(vel_ref[...], hid[...])
    mhalf[...] = jnp.zeros(mhalf.shape, F32)
    unpack(z)
    if H > 1:
        unpack((z + Z - 1) % Z)
        unpack((z + 1) % Z)
    loads[3].wait()
    readout = dot_t(vel_ref[...], aou_ref[...]).astype(BF16)
    for t in range(2, H):
        ring1(t)
        ring2(t)
        unpack((z + Z - t) % Z)
        unpack((z + t) % Z)
    last(wpiece, WPARTS, wr_recv)
    last(qpiece, 2, wq_recv, side)
    arrived(acols(xl, 0, 2), a_recv.at[3])
    arrived(acols(xl, 3, 1), a_recv.at[4])
    arrived(acols(xr, 0, 3), a_recv.at[5])
    arrived(acols(xo, 2, 1), a_recv.at[6])
    arrived(acols(xo, 3, 1), a_recv.at[7])
    for d in range(1, Y):
        arrived(yrows(xo, y), ay_recv.at[d])

    ZR = Z * R
    theirs = pl.ds(pl.multiple_of(2 * T * o, 16), 2 * T)
    mine = pl.ds(pl.multiple_of(2 * T * c, 16), 2 * T)
    for b in range(X):
        pacc[b * T : (b + 1) * T] = dot(acts[b, :, :ZR], wkv[0]) + dot(acts[b, :, ZR:], wkv[1])
    give = remote(pacc.at[theirs], precv, d_send.at[2], d_recv.at[2], other)
    give.start()

    give.wait_recv()
    kv[c, z] = (pacc[mine] + precv[...]).astype(BF16)

    def kpiece(zz, n):
        return kv.at[c, zz, pl.ds(n * (2 * T // KPARTS), 2 * T // KPARTS), :]

    def across(zz):
        s = remote(kv.at[c, zz], kv.at[c, zz], kd_send.at[zz], kd_recv.at[zz], other)
        s.start()
        return s

    kring = []
    cross = []

    def ring3(t):
        kring.extend(ring(kpiece, KPARTS, kr_send, kr_recv, t))
        cross.append(across((z + Z - t) % Z))
        if t:
            cross.append(across((z + t) % Z))

    ring3(0)
    unpack((z + H) % Z)
    givem = remote(mhalf, mrecv, d_send.at[3], d_recv.at[3], other)
    givem.start()

    for b in range(X):
        qacc[b * T : (b + 1) * T, :HEAD] = dot(acts[b, :, :ZR], wqb[0]) + dot(acts[b, :, ZR:], wqb[1])
        qacc[b * T : (b + 1) * T, HEAD:] = dot(acts[b, :, :ZR], wlow[0]) + dot(acts[b, :, ZR:], wlow[1])
    giveq = remote(qacc.at[theirs], qrecv, d_send.at[4], d_recv.at[4], other)
    giveq.start()
    if H > 1:
        ring3(1)
    up.wait()
    od.wait()
    givem.wait()
    mixw = mhalf[...] + mrecv[...]
    mix = mixw.astype(BF16)
    at = pl.ds(pl.multiple_of(HEAD * (x % 2), HEAD), HEAD)
    fmix = (mixw + dot_t(readout, aod_all[x // 2, at, :])).astype(BF16)
    zero = jnp.zeros_like(mix)
    mix = jnp.concatenate([mix, zero], axis=0)
    fmix = jnp.concatenate([zero, fmix], axis=0)
    giveq.wait()
    qsum = qacc[mine] + qrecv[...]
    lrows = pl.ds(pl.multiple_of(LC * y, 16), LC)
    loraT[lrows, :] = qsum[:, HEAD:].T[:LC].astype(BF16)
    for d in range(1, Y):
        s = remote(loraT.at[lrows], loraT.at[lrows], lo_send.at[d], lo_recv.at[d], dev(x, (y + d) % Y, z, c))
        s.start()
        sends.append(s)
    logit = HEAD ** (-0.5)
    q2[: 2 * T] = (qsum[:, :HEAD] * logit).astype(BF16)
    top_ref[...] = jnp.full(top_ref.shape, -jnp.inf, F32)
    sum_ref[...] = jnp.zeros(sum_ref.shape, F32)
    acc_ref[...] = jnp.zeros(acc_ref.shape, F32)

    def attend(cc, zz):
        for st in range(2):
            rows = slice(2 * T * st, 2 * T * (st + 1))
            s = dot_t(q2[rows], kv[cc, zz, :, :HEAD])
            best = s[:, :HEAD]
            for g in range(1, 2 * T // HEAD):
                best = jnp.maximum(best, s[:, g * HEAD : (g + 1) * HEAD])
            old = top_ref[rows]
            new = jnp.maximum(old, jnp.max(best, axis=1, keepdims=True))
            fade = jnp.exp(old - new)
            ps = [jnp.exp(s[:, g * HEAD : (g + 1) * HEAD] - new) for g in range(2 * T // HEAD)]
            l = sum_ref[rows] * fade
            for p in ps:
                l = l + p
            sum_ref[rows] = l
            top_ref[rows] = new
            probs = jnp.concatenate([p.astype(BF16) for p in ps], axis=1)
            acc_ref[rows] = acc_ref[rows] * fade + dot(probs, kv[cc, zz, :, HEAD:])

    def attend_both(zz):
        attend(c, zz)
        arrived(kv.at[o, zz], kd_recv.at[zz])
        attend(o, zz)

    for t in range(1, H):
        if t > 1:
            ring3(t)
        if t == min(2, H - 1):
            for d in range(1, Y):
                arrived(loraT.at[lrows], lo_recv.at[d])
            delta = lax.dot_general(
                loraT[...], aup_all[x // 2, :, at], (((0,), (0,)), ((), ())), preferred_element_type=F32
            )
            q2[2 * T :] = ((qsum[:, :HEAD] + delta) * logit).astype(BF16)
            attend_both(z)
        if t > 1:
            attend_both((z + Z - t + 1) % Z)
            attend_both((z + t - 1) % Z)
    if H == 1:
        for d in range(1, Y):
            arrived(loraT.at[lrows], lo_recv.at[d])
        delta = lax.dot_general(
            loraT[...], aup_all[x // 2, :, at], (((0,), (0,)), ((), ())), preferred_element_type=F32
        )
        q2[2 * T :] = ((qsum[:, :HEAD] + delta) * logit).astype(BF16)
        attend_both(z)
    else:
        attend_both((z + Z - H + 1) % Z)
        attend_both((z + H - 1) % Z)
    last(kpiece, KPARTS, kr_recv)
    cross.append(across((z + H) % Z))
    attend_both((z + H) % Z)

    attn = (acc_ref[...] / jnp.sum(sum_ref[...], axis=1, keepdims=True)).astype(BF16)
    part[...] = dot_t(attn[: 2 * T], mix) + dot_t(attn[2 * T :], fmix)

    slot = x * Y + y
    pos = 2 * y + c
    for d in range(1, 2 * Y):
        p = (pos + d) % (2 * Y)
        for b in range(2):
            src = part.at[pl.ds(pl.multiple_of(b * T + p * PT, 8), PT), :]
            remote(src, red.at[slot], red_send, red_recv, dev(2 * c + b, p // 2, z, p % 2)).start()

    def own(b):
        src = part.at[pl.ds(pl.multiple_of(b * T + pos * PT, 8), PT), :]
        away = remote(src, red.at[slot], own_send.at[b], red_recv, dev(2 * c + b, y, z, c))
        return away, pltpu.make_async_copy(src, red.at[slot], red_recv)

    for b in range(2):

        @pl.when(2 * c + b != x)
        def _():
            own(b)[0].start()

        @pl.when(2 * c + b == x)
        def _():
            own(b)[1].start()

    for i in range(2):
        j = 2 * c + i
        for n, (src, dst) in enumerate(exchange(i)):

            @pl.when(j != x)
            def _():
                remote(src, dst, xs_send.at[i, n], xs_recv.at[xslot, n], dev(j, y, z, x // 2)).wait_send()

    give.wait_send()
    for s in sends + wring + kring + cross:
        s.wait_send()
    arrived(red, red_recv)
    acc = red[0]
    for n in range(1, X * Y):
        acc = acc + red[n]
    err[0] = acc
    for d in range(1, 2 * Y):
        p = (pos + d) % (2 * Y)
        remote(err.at[0], fin.at[2 * Y - d], fin_send, fin_recv, dev(x, p // 2, z, p % 2)).start()
    fin[0] = acc
    for b in range(2):

        @pl.when(2 * c + b != x)
        def _():
            own(b)[0].wait_send()

    arrived(red.at[pl.ds(0, 4 * Y - 2)], red_send)
    arrived(fin.at[pl.ds(1, 2 * Y - 1)], fin_recv)
    sums = jnp.concatenate([fin[(n + 2 * Y - pos) % (2 * Y)] for n in range(2 * Y)], axis=0).T
    x0_real = noisy_wide - sigma * (baseT + sums[:C])
    x0_fake = noisy_wide - sigma * (baseT + sums[C:])
    gap = jnp.abs(lat_ref[...].astype(F32) - x0_real)
    err[1, 0:8] = jnp.sum(gap.reshape(C // 8, 8, T), axis=0)
    errs[0] = err[1, 0:8]
    S = X * Z
    for d in range(1, S):
        where = {"group": group, "seq": (seq + d) % S, "head": hd}
        remote(err.at[1, pl.ds(0, 8)], errs.at[d], err_send, err_recv, where).start()
    arrived(fin.at[pl.ds(1, 2 * Y - 1)], fin_send)
    arrived(errs.at[pl.ds(1, S - 1)], err_recv)
    tot = errs[0]
    for n in range(1, S):
        tot = tot + errs[n]
    tot = jnp.sum(jnp.sum(tot, axis=0, keepdims=True), axis=1, keepdims=True)
    weight = tot / (T * S * C)
    out_ref[...] = (x0_fake - x0_real) / weight

    arrived(errs.at[pl.ds(1, S - 1)], err_send)


def local(
    latents, noise, step, stream, patch_embed_weight, prenorm_gain_vector, query_matrix,
    key_matrix, value_matrix, output_matrix, velocity_readout_weight, adapter_query_down,
    adapter_query_up, adapter_output_down, adapter_output_up, *, dims,
):
    Y, Z, YL = dims
    T, D = stream.shape
    C = latents.shape[1]
    R = query_matrix.shape[0]
    PT = T // (2 * Y)
    H = Z // 2
    vmem = pl.BlockSpec(memory_space=pltpu.VMEM)
    hbm = pl.BlockSpec(memory_space=pl.ANY)
    dma = pltpu.SemaphoreType.DMA
    out = pl.pallas_call(
        functools.partial(kernel, dims),
        out_shape=jax.ShapeDtypeStruct((C, T), F32),
        in_specs=[pl.BlockSpec(memory_space=pltpu.SMEM), vmem, vmem, hbm, hbm] + [vmem] * 5 + [hbm] + [vmem] * 3 + [hbm],
        out_specs=vmem,
        scratch_shapes=[
            pltpu.VMEM((T, D), BF16),
            pltpu.VMEM((C, D), BF16),
            pltpu.VMEM((C, D), BF16),
            pltpu.VMEM((HEAD, D), BF16),
            pltpu.VMEM((T, D), BF16),
            pltpu.VMEM((X, T, D // 2), BF16),
            pltpu.VMEM((2, Z * R, 2 * HEAD), BF16),
            pltpu.VMEM((2, Z * R, HEAD), BF16),
            pltpu.VMEM((Z, 64 + C, HEAD), BF16),
            pltpu.VMEM((2, Z * R, HEAD), BF16),
            pltpu.VMEM((32, HEAD), BF16),
            pltpu.VMEM((2, C, HEAD), F32),
            pltpu.VMEM((2, C, HEAD), F32),
            pltpu.VMEM((2, HEAD, 2 * HEAD), BF16),
            pltpu.VMEM((2, 2 * HEAD, HEAD), BF16),
            pltpu.VMEM((X * T, 2 * HEAD), F32),
            pltpu.VMEM((2 * T, 2 * HEAD), F32),
            pltpu.VMEM((X * T, 2 * HEAD), F32),
            pltpu.VMEM((2 * T, 2 * HEAD), F32),
            pltpu.VMEM((C, HEAD), F32),
            pltpu.VMEM((C, HEAD), F32),
            pltpu.VMEM((HEAD, 2 * T), BF16),
            pltpu.VMEM((2, Z, 2 * T, 2 * HEAD), BF16),
            pltpu.VMEM((4 * T, HEAD), BF16),
            pltpu.VMEM((4 * T, HEAD), F32),
            pltpu.VMEM((4 * T, HEAD), F32),
            pltpu.VMEM((4 * T, HEAD), F32),
            pltpu.VMEM((2 * T, 2 * C), F32),
            pltpu.VMEM((X * Y, PT, 2 * C), F32),
            pltpu.VMEM((2 * Y, PT, 2 * C), F32),
            pltpu.VMEM((2, PT, 2 * C), F32),
            pltpu.VMEM((X * Z, 8, 2 * C), F32),
            dma((4,)),
            dma((2, 5)), dma((2, 5)),
            dma((8,)), dma((8,)),
            dma((Y,)), dma((Y,)),
            dma((2, H, WPARTS)), dma((2, H, WPARTS)),
            dma((2, H, 2)), dma((2, H, 2)),
            dma((2, H)), dma((2, H)),
            dma((5,)), dma((5,)),
            dma((Y,)), dma((Y,)),
            dma((2, H, KPARTS)), dma((2, H, KPARTS)),
            dma((Z,)), dma((Z,)),
            dma, dma, dma((2,)),
            dma, dma,
            dma, dma,
        ],
        compiler_params=pltpu.CompilerParams(
            collective_id=0, has_side_effects=True, vmem_limit_bytes=56 * 1024 * 1024
        ),
    )(
        step, latents.T, noise.T, stream, patch_embed_weight, prenorm_gain_vector.reshape(1, D),
        query_matrix, key_matrix, value_matrix, output_matrix.T, velocity_readout_weight,
        adapter_query_down, adapter_query_up, adapter_output_down, adapter_output_up,
    )
    return out.T


def solution(mesh):
    heads = ("group", "head")
    in_specs = (
        P("seq", None), P("seq", None), P(), P("seq", None), P(), P(),
        P("seq", heads), P("seq", heads), P("seq", heads), P(heads, "seq"),
        P(), P("seq", None), P(None, heads), P(heads, None), P(),
    )
    YL = mesh.shape["head"] // 2
    dims = (mesh.shape["group"] * YL, mesh.shape["seq"] // X, YL)
    return jax.shard_map(
        functools.partial(local, dims=dims), mesh=mesh, in_specs=in_specs,
        out_specs=P("seq", None), check_vma=False,
    )
```

```python
import functools

import jax
import jax.numpy as jnp
from jax import lax
from jax.experimental import pallas as pl
from jax.experimental.pallas import tpu as pltpu
from jax.sharding import PartitionSpec as P

HEAD = 128
X = 4
MESH = pl.DeviceIdType.MESH
BF16 = jnp.bfloat16
F32 = jnp.float32


def dot_t(left, right):
    return lax.dot_general(
        left, right, (((1,), (1,)), ((), ())), preferred_element_type=F32
    )


def dot(left, right):
    return jnp.dot(left, right, preferred_element_type=F32)


WPARTS = 2
KPARTS = 2


def kernel(
    dims,
    step_ref,
    lat_ref,
    noise_ref,
    stream_hbm,
    pe_hbm,
    gain_ref,
    wq_ref,
    wk_ref,
    wv_ref,
    om_ref,
    vel_hbm,
    ad_ref,
    aup_ref,
    aod_ref,
    aou_hbm,
    out_ref,
    stream_ref,
    pe_ref,
    vel_ref,
    aou_ref,
    hid,
    acts,
    wkv,
    wqb,
    ext,
    wlow,
    lpack,
    mpart,
    mpair,
    aup_all,
    aod_all,
    pacc,
    precv,
    qacc,
    qrecv,
    mhalf,
    mrecv,
    loraT,
    kv,
    q2,
    top_ref,
    sum_ref,
    acc_ref,
    part,
    red,
    fin,
    err,
    errs,
    load_sem,
    xs_send,
    xs_recv,
    a_send,
    a_recv,
    ay_send,
    ay_recv,
    wr_send,
    wr_recv,
    wq_send,
    wq_recv,
    we_send,
    we_recv,
    d_send,
    d_recv,
    lo_send,
    lo_recv,
    kr_send,
    kr_recv,
    kd_send,
    kd_recv,
    red_send,
    red_recv,
    own_send,
    fin_send,
    fin_recv,
    err_send,
    err_recv,
):
    Y, Z, YL = dims
    T, D = stream_ref.shape
    half = D // 2
    R = wq_ref.shape[0]
    C = lat_ref.shape[0]
    PT = T // (2 * Y)
    H = Z // 2
    G = R // 32
    LC = 16
    group = lax.axis_index("group")
    seq = lax.axis_index("seq")
    hd = lax.axis_index("head")
    y = group * YL + hd // 2
    c = hd % 2
    x = seq // Z
    z = seq % Z
    o = 1 - c

    def dev(xx, yy, zz, cc):
        return {"group": yy // YL, "seq": xx * Z + zz, "head": (yy % YL) * 2 + cc}

    def remote(src, dst, ssem, rsem, where):
        return pltpu.make_async_remote_copy(
            src_ref=src, dst_ref=dst, send_sem=ssem, recv_sem=rsem,
            device_id=where, device_id_type=MESH,
        )

    def arrived(ref, sem):
        pltpu.make_async_copy(ref, ref, sem).wait()

    loads = [
        pltpu.make_async_copy(src, dst, load_sem.at[n])
        for n, (src, dst) in enumerate(
            ((vel_hbm, vel_ref), (stream_hbm, stream_ref), (pe_hbm, pe_ref), (aou_hbm, aou_ref))
        )
    ]
    for l in loads:
        l.start()

    if LC * Y < HEAD:
        loraT[...] = jnp.zeros(loraT.shape, BF16)

    barrier = pltpu.get_barrier_semaphore()
    line = [dev(x, y, z, o)]
    for d in range(1, X):
        line += [dev((x + d) % X, y, z, c), dev((x + d) % X, y, z, o)]
    for d in range(1, Y):
        line += [dev(x, (y + d) % Y, z, c), dev(x, (y + d) % Y, z, o)]
    for d in range(1, Z):
        line.append(dev(x, y, (z + d) % Z, c))
    for where in line:
        pl.semaphore_signal(barrier, inc=1, device_id=where, device_id_type=MESH)

    loads[0].wait()
    lo = R * seq // 128
    window = vel_ref[:, pl.ds(pl.multiple_of(lo * 128, 128), 256)].astype(F32)
    off = R * seq - lo * 128
    turned = pltpu.roll(window, lax.rem(256 - off, 256), 1).astype(BF16)
    mp = dot(turned[:, :R], om_ref[...])
    mpart[0] = mp[:, :HEAD]
    mpart[1] = mp[:, HEAD:]

    low = pltpu.roll(ad_ref[...].astype(F32), lax.rem(128 - LC * y, 128), 1)
    lane = lax.broadcasted_iota(jnp.int32, (32, 128), 1)
    packed = jnp.zeros((32, 128), F32)
    for g in range(G):
        turned_low = low[32 * g : 32 * (g + 1)]
        if g:
            turned_low = pltpu.roll(turned_low, LC * g, 1)
        packed = jnp.where((lane >= LC * g) & (lane < LC * (g + 1)), turned_low, packed)
    lpack[...] = packed.astype(BF16)

    pl.semaphore_wait(barrier, len(line))

    xslot = x % 2
    myrows = pl.ds(pl.multiple_of(R * z, 16), R)

    def exchange(i):
        mine_ = pl.ds(HEAD * i, HEAD)
        return [
            (wk_ref.at[:, mine_], wkv.at[xslot, myrows, pl.ds(0, HEAD)]),
            (wv_ref.at[:, mine_], wkv.at[xslot, myrows, pl.ds(HEAD, HEAD)]),
            (wq_ref.at[:, mine_], wqb.at[xslot, myrows, :]),
            (lpack, ext.at[z, pl.ds(pl.multiple_of(32 * xslot, 16), 32), :]),
            (mpart.at[i], mpair.at[xslot]),
        ]

    both = exchange(0), exchange(1)
    for n in range(5):
        for i in range(2):
            j = 2 * c + i
            src, dst = both[i][n]

            @pl.when(j != x)
            def _():
                remote(src, dst, xs_send.at[i, n], xs_recv.at[xslot, n], dev(j, y, z, x // 2)).start()

            @pl.when(j == x)
            def _():
                pltpu.make_async_copy(src, dst, xs_recv.at[xslot, n]).start()

    other = dev(x, y, z, o)
    up = remote(aup_ref, aup_all.at[c], d_send.at[0], d_recv.at[0], other)
    od = remote(aod_ref, aod_all.at[c], d_send.at[1], d_recv.at[1], other)
    up.start()
    od.start()
    aup_all[c] = aup_ref[...]
    aod_all[c] = aod_ref[...]

    level = (jnp.full((1, 1), step_ref[0], jnp.int32).astype(F32) + 1.0) / 1000.0
    sigma = 5.0 * level / (1.0 + 4.0 * level)
    noisyT = ((1.0 - sigma) * lat_ref[...].astype(F32) + sigma * noise_ref[...].astype(F32)).astype(BF16)
    noisy_wide = noisyT.astype(F32)
    noisy = noisy_wide.T.astype(BF16)
    loads[1].wait()
    loads[2].wait()
    wide = 640 if D % 640 == 0 else D
    total = jnp.zeros((T, 1), F32)
    for k in range(D // wide):
        cols = slice(k * wide, (k + 1) * wide)
        h = (stream_ref[:, cols].astype(F32) + dot(noisy, pe_ref[:, cols])).astype(BF16)
        hid[:, cols] = h
        hw = h.astype(F32)
        total = total + jnp.sum(hw * hw, axis=1, keepdims=True)
    scale = lax.rsqrt(total / D + 1e-06)
    for k in range(half // wide):
        at = pl.ds(pl.multiple_of(c * half + k * wide, 128), wide)
        n = (hid[:, at].astype(F32) * scale * gain_ref[:, at]).astype(BF16)
        acts[x, :, k * wide : (k + 1) * wide] = n

    YT = T // Y
    Q4 = half // 4
    xo, xr, xl = (x + 2) % X, (x + 1) % X, (x + 3) % X

    def yrows(block, yy):
        return acts.at[block, pl.ds(pl.multiple_of(YT * yy, 16), YT), pl.ds(0, 2 * Q4)]

    def acols(block, lo_, n):
        return acts.at[block, :, pl.ds(lo_ * Q4, n * Q4)]

    sends = []

    def send_acts(ref, n, where):
        s = remote(ref, ref, a_send.at[n], a_recv.at[n], dev(where, y, z, c))
        s.start()
        sends.append(s)

    send_acts(yrows(x, y), 0, xo)
    send_acts(acols(x, 2, 1), 1, xr)
    send_acts(acols(x, 3, 1), 2, xl)
    send_acts(acols(x, 0, 2), 3, xr)
    send_acts(acols(x, 3, 1), 4, xr)
    send_acts(acols(x, 0, 3), 5, xl)

    right, left = dev(x, y, (z + 1) % Z, c), dev(x, y, (z + Z - 1) % Z, c)

    def ring(piece, parts, ssem, rsem, t, extra=None):
        turns = [
            (piece(((z + Z - t) % Z, (z + t) % Z)[way], n), way, ssem.at[way, t, n], rsem.at[way, t, n],
             rsem.at[way, t - 1, n] if t else None, t < H - 1 or n // (parts // 2) == way)
            for n in range(parts)
            for way in range(2)
        ]
        if extra is not None:
            ebox, es, er = extra
            turns[2:2] = [
                (ebox(((z + Z - t) % Z, (z + t) % Z)[way], 0), way, es.at[way, t], er.at[way, t],
                 er.at[way, t - 1] if t else None, t < H - 1 or way == 0)
                for way in range(2)
            ]
        started = []
        for ref, way, ss, rs, before, goes in turns:
            if goes:
                if t:
                    arrived(ref, before)
                s = remote(ref, ref, ss, rs, (right, left)[way])
                s.start()
                started.append(s)
        for ref, way, ss, rs, before, goes in turns:
            if t and not goes:
                arrived(ref, before)
        return started

    def last(piece, parts, rsem, extra=None):
        zz = (z + H) % Z
        for n in range(parts):
            arrived(piece(zz, n), rsem.at[n // (parts // 2), H - 1, n])
        if extra is not None:
            arrived(extra[0](zz, 0), extra[2].at[0, H - 1])

    def wpiece(zz, n):
        return wkv.at[n, pl.ds(pl.multiple_of(R * zz, 16), R), :]

    def qpiece(zz, n):
        return wqb.at[n, pl.ds(pl.multiple_of(R * zz, 16), R), :]

    def epiece(zz, n):
        return ext.at[zz]

    side = (epiece, we_send, we_recv)
    wring = []

    def ring1(t):
        wring.extend(ring(wpiece, WPARTS, wr_send, wr_recv, t))

    def ring2(t):
        wring.extend(ring(qpiece, 2, wq_send, wq_recv, t, side))

    def unpack(zz):
        for s in range(2):
            piece = ext[zz, 32 * s : 32 * (s + 1)].astype(F32)
            for g in range(G):
                rows = pltpu.roll(piece, 128 - LC * g, 1) if g else piece
                wlow[s, pl.ds(pl.multiple_of(R * zz + 32 * g, 16), 32), :] = rows.astype(BF16)
        mhalf[...] += ext[zz, 64 : 64 + C].astype(F32)

    for s in range(2):
        for n in range(2):
            arrived(wkv.at[s, myrows, pl.ds(HEAD * n, HEAD)], xs_recv.at[s, n])
    ring1(0)
    for s in range(2):
        arrived(wqb.at[s, myrows, :], xs_recv.at[s, 2])
        arrived(ext.at[z, pl.ds(32 * s, 32), :], xs_recv.at[s, 3])
        arrived(mpair.at[s], xs_recv.at[s, 4])
    ext[z, 64 : 64 + C] = (mpair[0] + mpair[1]).astype(BF16)

    ring2(0)
    arrived(yrows(xo, y), a_recv.at[0])
    for d in range(1, Y):
        s = remote(yrows(xo, y), yrows(xo, y), ay_send.at[d], ay_recv.at[d], dev(x, (y + d) % Y, z, c))
        s.start()
        sends.append(s)
    if H > 1:
        ring1(1)
    arrived(acols(xl, 2, 1), a_recv.at[1])
    send_acts(acols(xl, 2, 1), 6, xr)
    arrived(acols(xr, 3, 1), a_recv.at[2])
    send_acts(acols(xr, 3, 1), 7, xl)
    if H > 1:
        ring2(1)
    baseT = dot_t(vel_ref[...], hid[...])
    mhalf[...] = jnp.zeros(mhalf.shape, F32)
    unpack(z)
    if H > 1:
        unpack((z + Z - 1) % Z)
        unpack((z + 1) % Z)
    loads[3].wait()
    readout = dot_t(vel_ref[...], aou_ref[...]).astype(BF16)
    for t in range(2, H):
        ring1(t)
        ring2(t)
        unpack((z + Z - t) % Z)
        unpack((z + t) % Z)
    last(wpiece, WPARTS, wr_recv)
    last(qpiece, 2, wq_recv, side)
    arrived(acols(xl, 0, 2), a_recv.at[3])
    arrived(acols(xl, 3, 1), a_recv.at[4])
    arrived(acols(xr, 0, 3), a_recv.at[5])
    arrived(acols(xo, 2, 1), a_recv.at[6])
    arrived(acols(xo, 3, 1), a_recv.at[7])
    for d in range(1, Y):
        arrived(yrows(xo, y), ay_recv.at[d])

    ZR = Z * R
    theirs = pl.ds(pl.multiple_of(2 * T * o, 16), 2 * T)
    mine = pl.ds(pl.multiple_of(2 * T * c, 16), 2 * T)
    for b in range(X):
        pacc[b * T : (b + 1) * T] = dot(acts[b, :, :ZR], wkv[0]) + dot(acts[b, :, ZR:], wkv[1])
    give = remote(pacc.at[theirs], precv, d_send.at[2], d_recv.at[2], other)
    give.start()

    give.wait_recv()
    kv[c, z] = (pacc[mine] + precv[...]).astype(BF16)

    def kpiece(zz, n):
        return kv.at[c, zz, pl.ds(n * (2 * T // KPARTS), 2 * T // KPARTS), :]

    def across(zz):
        s = remote(kv.at[c, zz], kv.at[c, zz], kd_send.at[zz], kd_recv.at[zz], other)
        s.start()
        return s

    kring = []
    cross = []

    def ring3(t):
        kring.extend(ring(kpiece, KPARTS, kr_send, kr_recv, t))
        cross.append(across((z + Z - t) % Z))
        if t:
            cross.append(across((z + t) % Z))

    ring3(0)
    unpack((z + H) % Z)
    givem = remote(mhalf, mrecv, d_send.at[3], d_recv.at[3], other)
    givem.start()

    for b in range(X):
        qacc[b * T : (b + 1) * T, :HEAD] = dot(acts[b, :, :ZR], wqb[0]) + dot(acts[b, :, ZR:], wqb[1])
        qacc[b * T : (b + 1) * T, HEAD:] = dot(acts[b, :, :ZR], wlow[0]) + dot(acts[b, :, ZR:], wlow[1])
    giveq = remote(qacc.at[theirs], qrecv, d_send.at[4], d_recv.at[4], other)
    giveq.start()
    if H > 1:
        ring3(1)
    up.wait()
    od.wait()
    givem.wait()
    mixw = mhalf[...] + mrecv[...]
    mix = mixw.astype(BF16)
    at = pl.ds(pl.multiple_of(HEAD * (x % 2), HEAD), HEAD)
    fmix = (mixw + dot_t(readout, aod_all[x // 2, at, :])).astype(BF16)
    zero = jnp.zeros_like(mix)
    mix = jnp.concatenate([mix, zero], axis=0)
    fmix = jnp.concatenate([zero, fmix], axis=0)
    giveq.wait()
    qsum = qacc[mine] + qrecv[...]
    lrows = pl.ds(pl.multiple_of(LC * y, 16), LC)
    loraT[lrows, :] = qsum[:, HEAD:].T[:LC].astype(BF16)
    for d in range(1, Y):
        s = remote(loraT.at[lrows], loraT.at[lrows], lo_send.at[d], lo_recv.at[d], dev(x, (y + d) % Y, z, c))
        s.start()
        sends.append(s)
    logit = HEAD ** (-0.5)
    q2[: 2 * T] = (qsum[:, :HEAD] * logit).astype(BF16)
    top_ref[...] = jnp.full(top_ref.shape, -jnp.inf, F32)
    sum_ref[...] = jnp.zeros(sum_ref.shape, F32)
    acc_ref[...] = jnp.zeros(acc_ref.shape, F32)

    def attend_both(zz):
        arrived(kv.at[o, zz], kd_recv.at[zz])
        for st in range(2):
            rows = slice(2 * T * st, 2 * T * (st + 1))
            s = dot_t(q2[rows], kv[:, zz, :, :HEAD].reshape(4 * T, HEAD))
            best = s[:, :HEAD]
            for g in range(1, 4 * T // HEAD):
                best = jnp.maximum(best, s[:, g * HEAD : (g + 1) * HEAD])
            old = top_ref[rows]
            new = jnp.maximum(old, jnp.max(best, axis=1, keepdims=True))
            fade = jnp.exp(old - new)
            ps = [jnp.exp(s[:, g * HEAD : (g + 1) * HEAD] - new) for g in range(4 * T // HEAD)]
            l = sum_ref[rows] * fade
            for p in ps:
                l = l + p
            sum_ref[rows] = l
            top_ref[rows] = new
            probs = jnp.concatenate([p.astype(BF16) for p in ps], axis=1)
            acc_ref[rows] = acc_ref[rows] * fade + dot(probs, kv[:, zz, :, HEAD:].reshape(4 * T, HEAD))

    for t in range(1, H):
        if t > 1:
            ring3(t)
        if t == min(2, H - 1):
            for d in range(1, Y):
                arrived(loraT.at[lrows], lo_recv.at[d])
            delta = lax.dot_general(
                loraT[...], aup_all[x // 2, :, at], (((0,), (0,)), ((), ())), preferred_element_type=F32
            )
            q2[2 * T :] = ((qsum[:, :HEAD] + delta) * logit).astype(BF16)
            attend_both(z)
        if t > 1:
            attend_both((z + Z - t + 1) % Z)
            attend_both((z + t - 1) % Z)
    if H == 1:
        for d in range(1, Y):
            arrived(loraT.at[lrows], lo_recv.at[d])
        delta = lax.dot_general(
            loraT[...], aup_all[x // 2, :, at], (((0,), (0,)), ((), ())), preferred_element_type=F32
        )
        q2[2 * T :] = ((qsum[:, :HEAD] + delta) * logit).astype(BF16)
        attend_both(z)
    else:
        attend_both((z + Z - H + 1) % Z)
        attend_both((z + H - 1) % Z)
    last(kpiece, KPARTS, kr_recv)
    cross.append(across((z + H) % Z))
    attend_both((z + H) % Z)

    attn = (acc_ref[...] / jnp.sum(sum_ref[...], axis=1, keepdims=True)).astype(BF16)
    part[...] = dot_t(attn[: 2 * T], mix) + dot_t(attn[2 * T :], fmix)

    slot = x * Y + y
    pos = 2 * y + c
    for d in range(1, 2 * Y):
        p = (pos + d) % (2 * Y)
        for b in range(2):
            src = part.at[pl.ds(pl.multiple_of(b * T + p * PT, 8), PT), :]
            remote(src, red.at[slot], red_send, red_recv, dev(2 * c + b, p // 2, z, p % 2)).start()

    def own(b):
        src = part.at[pl.ds(pl.multiple_of(b * T + pos * PT, 8), PT), :]
        away = remote(src, red.at[slot], own_send.at[b], red_recv, dev(2 * c + b, y, z, c))
        return away, pltpu.make_async_copy(src, red.at[slot], red_recv)

    for b in range(2):

        @pl.when(2 * c + b != x)
        def _():
            own(b)[0].start()

        @pl.when(2 * c + b == x)
        def _():
            own(b)[1].start()

    for i in range(2):
        j = 2 * c + i
        for n, (src, dst) in enumerate(exchange(i)):

            @pl.when(j != x)
            def _():
                remote(src, dst, xs_send.at[i, n], xs_recv.at[xslot, n], dev(j, y, z, x // 2)).wait_send()

    give.wait_send()
    for s in sends + wring + kring + cross:
        s.wait_send()
    arrived(red, red_recv)
    acc = red[0]
    for n in range(1, X * Y):
        acc = acc + red[n]
    err[0] = acc
    for d in range(1, 2 * Y):
        p = (pos + d) % (2 * Y)
        remote(err.at[0], fin.at[2 * Y - d], fin_send, fin_recv, dev(x, p // 2, z, p % 2)).start()
    fin[0] = acc
    for b in range(2):

        @pl.when(2 * c + b != x)
        def _():
            own(b)[0].wait_send()

    arrived(red.at[pl.ds(0, 4 * Y - 2)], red_send)
    arrived(fin.at[pl.ds(1, 2 * Y - 1)], fin_recv)
    sums = jnp.concatenate([fin[(n + 2 * Y - pos) % (2 * Y)] for n in range(2 * Y)], axis=0).T
    x0_real = noisy_wide - sigma * (baseT + sums[:C])
    x0_fake = noisy_wide - sigma * (baseT + sums[C:])
    gap = jnp.abs(lat_ref[...].astype(F32) - x0_real)
    err[1, 0:8] = jnp.sum(gap.reshape(C // 8, 8, T), axis=0)
    errs[0] = err[1, 0:8]
    S = X * Z
    for d in range(1, S):
        where = {"group": group, "seq": (seq + d) % S, "head": hd}
        remote(err.at[1, pl.ds(0, 8)], errs.at[d], err_send, err_recv, where).start()
    arrived(fin.at[pl.ds(1, 2 * Y - 1)], fin_send)
    arrived(errs.at[pl.ds(1, S - 1)], err_recv)
    tot = errs[0]
    for n in range(1, S):
        tot = tot + errs[n]
    tot = jnp.sum(jnp.sum(tot, axis=0, keepdims=True), axis=1, keepdims=True)
    weight = tot / (T * S * C)
    out_ref[...] = (x0_fake - x0_real) / weight

    arrived(errs.at[pl.ds(1, S - 1)], err_send)


def local(
    latents, noise, step, stream, patch_embed_weight, prenorm_gain_vector, query_matrix,
    key_matrix, value_matrix, output_matrix, velocity_readout_weight, adapter_query_down,
    adapter_query_up, adapter_output_down, adapter_output_up, *, dims,
):
    Y, Z, YL = dims
    T, D = stream.shape
    C = latents.shape[1]
    R = query_matrix.shape[0]
    PT = T // (2 * Y)
    H = Z // 2
    vmem = pl.BlockSpec(memory_space=pltpu.VMEM)
    hbm = pl.BlockSpec(memory_space=pl.ANY)
    dma = pltpu.SemaphoreType.DMA
    out = pl.pallas_call(
        functools.partial(kernel, dims),
        out_shape=jax.ShapeDtypeStruct((C, T), F32),
        in_specs=[pl.BlockSpec(memory_space=pltpu.SMEM), vmem, vmem, hbm, hbm] + [vmem] * 5 + [hbm] + [vmem] * 3 + [hbm],
        out_specs=vmem,
        scratch_shapes=[
            pltpu.VMEM((T, D), BF16),
            pltpu.VMEM((C, D), BF16),
            pltpu.VMEM((C, D), BF16),
            pltpu.VMEM((HEAD, D), BF16),
            pltpu.VMEM((T, D), BF16),
            pltpu.VMEM((X, T, D // 2), BF16),
            pltpu.VMEM((2, Z * R, 2 * HEAD), BF16),
            pltpu.VMEM((2, Z * R, HEAD), BF16),
            pltpu.VMEM((Z, 64 + C, HEAD), BF16),
            pltpu.VMEM((2, Z * R, HEAD), BF16),
            pltpu.VMEM((32, HEAD), BF16),
            pltpu.VMEM((2, C, HEAD), F32),
            pltpu.VMEM((2, C, HEAD), F32),
            pltpu.VMEM((2, HEAD, 2 * HEAD), BF16),
            pltpu.VMEM((2, 2 * HEAD, HEAD), BF16),
            pltpu.VMEM((X * T, 2 * HEAD), F32),
            pltpu.VMEM((2 * T, 2 * HEAD), F32),
            pltpu.VMEM((X * T, 2 * HEAD), F32),
            pltpu.VMEM((2 * T, 2 * HEAD), F32),
            pltpu.VMEM((C, HEAD), F32),
            pltpu.VMEM((C, HEAD), F32),
            pltpu.VMEM((HEAD, 2 * T), BF16),
            pltpu.VMEM((2, Z, 2 * T, 2 * HEAD), BF16),
            pltpu.VMEM((4 * T, HEAD), BF16),
            pltpu.VMEM((4 * T, HEAD), F32),
            pltpu.VMEM((4 * T, HEAD), F32),
            pltpu.VMEM((4 * T, HEAD), F32),
            pltpu.VMEM((2 * T, 2 * C), F32),
            pltpu.VMEM((X * Y, PT, 2 * C), F32),
            pltpu.VMEM((2 * Y, PT, 2 * C), F32),
            pltpu.VMEM((2, PT, 2 * C), F32),
            pltpu.VMEM((X * Z, 8, 2 * C), F32),
            dma((4,)),
            dma((2, 5)), dma((2, 5)),
            dma((8,)), dma((8,)),
            dma((Y,)), dma((Y,)),
            dma((2, H, WPARTS)), dma((2, H, WPARTS)),
            dma((2, H, 2)), dma((2, H, 2)),
            dma((2, H)), dma((2, H)),
            dma((5,)), dma((5,)),
            dma((Y,)), dma((Y,)),
            dma((2, H, KPARTS)), dma((2, H, KPARTS)),
            dma((Z,)), dma((Z,)),
            dma, dma, dma((2,)),
            dma, dma,
            dma, dma,
        ],
        compiler_params=pltpu.CompilerParams(
            collective_id=0, has_side_effects=True, vmem_limit_bytes=56 * 1024 * 1024
        ),
    )(
        step, latents.T, noise.T, stream, patch_embed_weight, prenorm_gain_vector.reshape(1, D),
        query_matrix, key_matrix, value_matrix, output_matrix.T, velocity_readout_weight,
        adapter_query_down, adapter_query_up, adapter_output_down, adapter_output_up,
    )
    return out.T


def solution(mesh):
    heads = ("group", "head")
    in_specs = (
        P("seq", None), P("seq", None), P(), P("seq", None), P(), P(),
        P("seq", heads), P("seq", heads), P("seq", heads), P(heads, "seq"),
        P(), P("seq", None), P(None, heads), P(heads, None), P(),
    )
    YL = mesh.shape["head"] // 2
    dims = (mesh.shape["group"] * YL, mesh.shape["seq"] // X, YL)
    return jax.shard_map(
        functools.partial(local, dims=dims), mesh=mesh, in_specs=in_specs,
        out_specs=P("seq", None), check_vma=False,
    )
```
